128 devices in a mesh: section: 4 (over z), tensor: 8 (over y_lo, x), dp: 4 (over y_hi, core).
Axes of the slice: x: 4, y: 4 (y_hi: 2, y_lo: 2; y = y_hi * 2 + y_lo), z: 4, core: 2. Of those that a mesh axis runs over, the one named last changes fastest.
Arguments:
- weights: bfloat16 [4, 8192, 8192], P('section', None, 'tensor'), may hold values from -0.0625 to 0.0625
- acts: bfloat16 [4, 4, 256, 8192], P('section', None, 'dp', 'tensor'), may hold values from -0.1875 to 0.1875
- gates: bfloat16 [4, 4, 256, 8192], P('section', None, 'dp', 'tensor'), may hold values from 0.25 to 1.75
- out_grad: bfloat16 [4, 256, 8192], P(None, 'dp', 'tensor'), may hold values from -6 to 6
- owner_rows: int32 [4, 4], replicated, may hold values from 8 to 24, as said below
Outputs:
- owned_grad: bfloat16 [4, 4, 3072, 8192], P('section', 'dp', None, 'tensor')
- section_grads: bfloat16 [4, 4, 256, 8192], P('section', None, 'dp', 'tensor')
The draws below stay inside these ranges and needn't reach their ends.
Inputs may be any that keep to these rules, and one draw needn't show every extreme that they name: `owner_rows`: each row sums to 64; owners take consecutive row ranges in dp order; in every section one owner holds exactly the maximum, and the first owner holds fewer than 16 blocks.
All inputs are finite; a program needn't handle non-finite values.
Results may differ from the reference program's by a relative error of at most 0.035.
Values may be sent and summed in bfloat16 or wider, within the bound.
A program may use at most 448 MiB of HBM per device.

```python
import jax
import jax.numpy as jnp
from jax import lax

E = 8192
MB = 4
TOK_MB = 64
OWN_BLK = 128
ROWS = 256
N_SECTION = 4
N_TENSOR = 8
N_DP = 4


def draw_owner_rows(key, part):
    key = jax.random.fold_in(key, 7)
    blocks = E // OWN_BLK
    most = 3 * E // (2 * N_DP * OWN_BLK)
    share = E // (N_DP * OWN_BLK)
    half_share = share // 2
    shrink = jax.random.randint(jax.random.fold_in(key, 100), (N_SECTION,), 0, half_share).astype(jnp.int32)
    first = (share - 1 - shrink).astype(jnp.int32)
    remain = (blocks - most - first).astype(jnp.int32)
    second = (remain // 2).astype(jnp.int32)
    third = (remain - second).astype(jnp.int32)
    columns = [first, second, third]
    position = jax.random.randint(jax.random.fold_in(key, 1), (N_SECTION,), 1, N_DP).astype(jnp.int32)
    zeros_col = jnp.zeros((N_SECTION,), jnp.int32)
    full = []
    for index in range(N_DP):
        before = columns[index] if index < N_DP - 1 else zeros_col
        after = columns[index - 1] if index >= 1 else zeros_col
        value = jnp.where(index == position, most, jnp.where(index < position, before, after))
        full.append(value.astype(jnp.int32))
    return jnp.stack(full, axis=1)


def shard_levels(key, extent, split, low, high):
    def one(dim, shards_of):
        steps = jax.random.uniform(jax.random.fold_in(jax.random.fold_in(key, 6), dim), (shards_of,), jnp.float32, low / len(split), high / len(split))
        return jnp.repeat(jnp.exp(steps), extent[dim] // shards_of).reshape((-1,) + (1,) * (len(extent) - dim - 1))

    level = one(*split[0])
    for cut in split[1:]:
        level = level * one(*cut)
    return level


def noise(own_key, dims, scale, reach, shards=(), kind=jnp.bfloat16):
    entries = scale * jax.random.normal(own_key, dims, jnp.float32)
    if shards:
        entries = entries * shard_levels(own_key, dims, shards, -0.22, 0.18)
    return jnp.clip(entries, -reach, reach).astype(kind)


def setup_inputs(seed: int = 0) -> dict:
    splits = jax.random.split(jax.random.key(seed), 6)
    return {
        "weights": noise(splits[0], (N_SECTION, E, E), E ** -0.5, 0.0625, ((0, 4), (2, 8))),
        "acts": noise(splits[1], (N_SECTION, MB, ROWS, E), ((MB * ROWS) ** -0.5), 0.1875, ((0, 4), (2, 4), (3, 8))),
        "gates": jnp.clip(0.25 + 1.5 * jax.random.uniform(splits[2], (N_SECTION, MB, ROWS, E), jnp.float32) ** shard_levels(splits[2], (N_SECTION, MB, ROWS, E), ((0, 4), (2, 4), (3, 8)), -0.2, 0.2), 0.25, 1.75).astype(jnp.bfloat16),
        "out_grad": noise(splits[3], (MB, ROWS, E), 1.0, 6.0, ((1, 4), (2, 8))),
        "owner_rows": draw_owner_rows(jax.random.fold_in(splits[5], 71), 0),
    }


def owner_blocks(weight_grad, counts, cap):
    width = weight_grad.shape[1]
    starts = (jnp.cumsum(counts) - counts).astype(jnp.int32)
    extended = jnp.concatenate([weight_grad, jnp.zeros((cap, width), jnp.bfloat16)], axis=0)
    blocks = []
    for owner in range(counts.shape[0]):
        piece = lax.dynamic_slice_in_dim(extended, starts[owner], cap, 0)
        keep = jnp.arange(cap)[:, None] < counts[owner]
        blocks.append(jnp.where(keep, piece, jnp.zeros_like(piece)))
    return jnp.stack(blocks)


def reference(weights, acts, gates, out_grad, owner_rows):
    width = weights.shape[1]
    group = width // N_TENSOR
    cap = 3 * width // (2 * N_DP)
    upstream = out_grad
    grads_list = []
    owned_list = []
    for section in range(N_SECTION - 1, -1, -1):
        pre_grad = (upstream.astype(jnp.float32) * gates[section].astype(jnp.float32)).astype(jnp.bfloat16)
        flat = pre_grad.reshape(-1, width)
        weight = weights[section]
        total = jnp.zeros((flat.shape[0], width), jnp.float32)
        for group_index in range(N_TENSOR):
            lower = group_index * group
            partial_value = jnp.dot(flat[:, lower:lower + group], weight[:, lower:lower + group].T, preferred_element_type=jnp.float32)
            total = total + partial_value.astype(jnp.bfloat16).astype(jnp.float32)
        section_grad = total.astype(jnp.bfloat16).reshape(upstream.shape)
        weight_grad = jnp.zeros((width, width), jnp.float32)
        for replica in range(N_DP):
            lower = replica * TOK_MB
            inputs_part = acts[section][:, lower:lower + TOK_MB].reshape(-1, width)
            grad_part = pre_grad[:, lower:lower + TOK_MB].reshape(-1, width)
            term = jnp.dot(inputs_part.T, grad_part, preferred_element_type=jnp.float32)
            weight_grad = weight_grad + term.astype(jnp.bfloat16).astype(jnp.float32)
        weight_grad = weight_grad.astype(jnp.bfloat16)
        counts = (owner_rows[section] * OWN_BLK).astype(jnp.int32)
        owned_list.insert(0, owner_blocks(weight_grad, counts, cap))
        grads_list.insert(0, section_grad)
        upstream = section_grad
    return jnp.stack(owned_list), jnp.stack(grads_list)
```

```python
import functools

import jax
import jax.numpy as jnp
from jax import lax
from jax.experimental import pallas as pl
from jax.experimental.pallas import tpu as pltpu
from jax.sharding import PartitionSpec as P

OWN_BLK = 128
STEPS = 8
MESH = pl.DeviceIdType.MESH
BF = jnp.bfloat16
F32 = jnp.float32


def remote(src, dst, sems, index, device):
    return pltpu.make_async_remote_copy(
        src_ref=src,
        dst_ref=dst,
        send_sem=sems.at[(0,) + index],
        recv_sem=sems.at[(1,) + index],
        device_id=device,
        device_id_type=MESH,
    )


def pipeline_kernel(
    weight, acts, gates, out_grad,
    grads, all_acts, all_pre,
    wv, gv, ov, uv, pv, part, got_a, got_b, got_u, got_y, kept, total,
    w_sem, in_sem, og_sem, pre_sem, a_sem, b_sem, u_sem, y_sem, ag_sem, fix_sem, loc_sem, out_loc_sem, out_sem, g_sem, sib_sem,
):
    section = lax.axis_index("section")
    tensor = lax.axis_index("tensor")
    dp = lax.axis_index("dp")
    last_section = lax.axis_size("section") - 1
    x, yl = lax.rem(tensor, 4), tensor // 4
    yh, core = dp // 2, lax.rem(dp, 2)
    y = yh * 2 + yl
    micro = 256 // STEPS
    half = 512

    def at(x_, y_, z_, core_):
        y_ = lax.rem(y_ + 4, 4)
        return (z_, lax.rem(y_, 2) * 4 + lax.rem(x_ + 4, 4), (y_ // 2) * 2 + core_)

    right, left = at(x + 1, y, section, core), at(x - 1, y, section, core)
    up, down = at(x, y + 1, section, core), at(x, y - 1, section, core)
    across = at(x, y + 2, section, core)
    sibling = at(x, y, section, 1 - core)
    other_y = yh * 2 + 1 - yl
    partner = at(x, other_y, section, core)
    below = lax.rem(section + last_section, last_section + 1)
    above = lax.rem(section + 1, last_section + 1)
    below_same, below_other = at(x, y, below, core), at(x, other_y, below, core)
    above_same, above_other = at(x, y, above, core), at(x, other_y, above, core)

    mine = pl.ds(pl.multiple_of(core * half, half), half)
    theirs = pl.ds(pl.multiple_of((1 - core) * half, half), half)

    places = (
        (2, 0), (2, 1), (1, 1), (3, 0), (1, 0), (3, 1), (0, 1 - yl), (0, yl),
    )
    loads = []
    for k, (dx, l) in enumerate(places):
        start = (l * 4 + lax.rem(x + dx, 4)) * 1024 + core * half
        load = pltpu.make_async_copy(
            weight.at[pl.ds(pl.multiple_of(start, half), half), :], wv.at[k], w_sem.at[k]
        )
        load.start()
        loads.append(load)
    own_gate = pltpu.make_async_copy(gates.at[:, mine], gv.at[core], loc_sem.at[0])
    own_gate.start()
    own_acts = pltpu.make_async_copy(acts, all_acts.at[y, x, core], loc_sem.at[1])
    own_acts.start()
    own_grad = pltpu.make_async_copy(out_grad.at[:, mine], ov.at[core], loc_sem.at[2])

    barrier = pltpu.get_barrier_semaphore()
    neighbours = (
        right, left, up, down, across, sibling, below_same, below_other, above_same, above_other,
    )
    for device in neighbours:
        pl.semaphore_signal(barrier, inc=1, device_id=device, device_id_type=MESH)
    pl.semaphore_wait(barrier, len(neighbours))

    gate_swap = remote(gates.at[:, theirs], gv.at[core], in_sem, (), sibling)
    gate_swap.start()
    grad_swap = remote(out_grad.at[:, theirs], ov.at[core], og_sem, (), sibling)

    @pl.when(section == last_section)
    def _():
        own_grad.start()
        grad_swap.start()

    lo, hi = pl.ds(0, 128), pl.ds(128, 128)
    lo_a, lo_b = pl.ds(0, 64), pl.ds(64, 64)
    hi_a, hi_b = pl.ds(128, 64), pl.ds(192, 64)
    xr, xl = lax.rem(x + 1, 4), lax.rem(x + 3, 4)
    yu, yd = lax.rem(y + 1, 4), lax.rem(y + 3, 4)

    def copy(k, src, dst, device):
        return remote(src, dst, g_sem, (k,), device)

    def same(k, ref, device):
        return copy(k, ref, ref, device)

    def sib(k, ref):
        return remote(ref, ref, sib_sem, (k,), sibling)

    def phase1():
        t_lo, t_hi = all_acts.at[y, x, core, lo], all_acts.at[y, x, core, hi]
        return [
            copy(0, acts.at[lo], t_lo, right), copy(1, acts.at[lo], t_lo, left),
            copy(2, acts.at[hi], t_hi, up), copy(3, acts.at[hi], t_hi, down),
        ]

    def phase2():
        return [
            same(4, all_acts.at[y, xl, core, lo_a], right), same(5, all_acts.at[y, xr, core, lo_b], left),
            same(6, all_acts.at[yd, x, core, hi_a], up), same(7, all_acts.at[yu, x, core, hi_b], down),
        ]

    def phase3():
        row, column = all_acts.at[y, :, core, lo], all_acts.at[:, x, core, hi]
        return [same(8, row, up), same(9, row, down), same(10, column, right), same(11, column, left),
                sib(0, row), sib(1, column)]

    def phase4():
        return [
            same(12, all_acts.at[yd, :, core, lo_a], up), same(13, all_acts.at[yu, :, core, lo_b], down),
            same(14, all_acts.at[:, xl, core, hi_a], right), same(15, all_acts.at[:, xr, core, hi_b], left),
            sib(2, all_acts.at[yd, :, core, lo]), sib(3, all_acts.at[yu, :, core, lo]),
            sib(4, all_acts.at[:, xl, core, hi]), sib(5, all_acts.at[:, xr, core, hi]),
        ]

    def phase5():
        return [sib(6, all_acts.at[lax.rem(y + 2, 4), :, core, lo]), sib(7, all_acts.at[:, lax.rem(x + 2, 4), core, hi])]

    phases = (phase1, phase2, phase3, phase4, phase5)
    arrivals = (4, 4, 4, 4, 0)
    early = (1, 1, 2, 3, 9)

    def run_phase(index):
        if index == 2:
            own_acts.wait()
        if index > 0:
            for c in phases[index - 1]()[: arrivals[index - 1]]:
                c.wait_recv()
        for c in phases[index]():
            c.start()

    def gather(before):
        for index in range(len(phases)):
            first = last_section - section >= early[index]
            pl.when(first if before else jnp.logical_not(first))(functools.partial(run_phase, index))

    gather(True)

    own_gate.wait()
    gate_swap.wait()

    @pl.when(section == last_section)
    def _():
        own_grad.wait()
        grad_swap.wait()

    def rows_of(m):
        return pl.ds(pl.multiple_of(m * micro, micro), micro)

    def pre_swap(m):
        ref = pv.at[:, rows_of(m), mine]
        return remote(ref, ref, pre_sem, (m,), sibling)

    def pre_across(m):
        return remote(pv.at[:, rows_of(m), mine], all_pre.at[yh, :, rows_of(m), mine], ag_sem, (m,), across)

    def send_a(m, k):
        return remote(part.at[m, k], got_a.at[m, k], a_sem, (m, k), (right, left)[k])

    def send_b(m, k):
        return remote(part.at[m, 2 + k], got_b.at[m, k], b_sem, (m, k), (right, left)[k % 2])

    def send_u(m, k):
        return remote((kept.at[m], part.at[m, 6])[k], got_u.at[m, k], u_sem, (m, k), (below_same, below_other)[k])

    def send_y(m):
        return remote(part.at[m, 6], got_y.at[m], y_sem, (m,), partner)

    def grad_own(m):
        return pltpu.make_async_copy(total.at[core, rows_of(m), :], grads.at[rows_of(m), mine], out_loc_sem.at[m])

    def grad_other(m):
        return remote(total.at[1 - core, rows_of(m), :], grads.at[rows_of(m), mine], out_sem, (m,), sibling)

    def product(m, k):
        pre = jnp.concatenate([pv[0, rows_of(m), :], pv[1, rows_of(m), :]], axis=0)
        w = wv[2 * k : 2 * k + 2].reshape(2 * half, 1024)
        value = lax.dot_general(pre, w, (((1,), (1,)), ((), ())), preferred_element_type=F32).astype(BF)
        part[m, 2 * k] = value[:, :half]
        part[m, 2 * k + 1] = value[:, half:]

    def add3(m, role, l):
        return (
            part[m, role].astype(F32) + got_b[m, 1 - l].astype(F32) + got_b[m, 2 + l].astype(F32)
        ).astype(BF)

    def reduce_step(m):
        for k in range(4):
            send_b(m, k).wait_recv()
        part[m, 6] = add3(m, 6, 1 - yl)

        @pl.when(section > 0)
        def _():
            send_u(m, 1).start()

        send_y(m).start()
        kept[m] = add3(m, 7, yl)

        @pl.when(section > 0)
        def _():
            send_u(m, 0).start()

    def finish_step(m):
        send_y(m).wait_recv()
        value = (kept[m].astype(F32) + got_y[m].astype(F32)).astype(BF)
        total[0, rows_of(m), :] = value[:micro]
        total[1, rows_of(m), :] = value[micro:]
        grad_own(m).start()
        grad_other(m).start()

    def step(m, _):
        @pl.when(section == last_section)
        def _():
            uv[...] = ov[:, rows_of(m), :]

        @pl.when(section < last_section)
        def _():
            send_u(m, 0).wait_recv()
            send_u(m, 1).wait_recv()
            value = (got_u[m, 0].astype(F32) + got_u[m, 1].astype(F32)).astype(BF)
            uv[0] = value[:micro]
            uv[1] = value[micro:]

        pre = (uv[...].astype(F32) * gv[:, rows_of(m), :].astype(F32)).astype(BF)
        pv[:, rows_of(m), mine] = pre
        pre_swap(m).start()
        pre_across(m).start()

        @pl.when(m > 1)
        def _():
            finish_step(m - 2)

        @pl.when(m == 0)
        def _():
            loads[0].wait()
            loads[1].wait()

        pre_swap(m).wait_recv()
        product(m, 0)
        send_a(m, 0).start()
        send_a(m, 1).start()

        @pl.when(m == 0)
        def _():
            loads[2].wait()
            loads[3].wait()

        product(m, 1)
        send_b(m, 0).start()
        send_b(m, 1).start()

        @pl.when(m > 0)
        def _():
            reduce_step(m - 1)

        @pl.when(m == 0)
        def _():
            for k in range(4, 8):
                loads[k].wait()

        product(m, 2)
        for k in range(2):
            send_a(m, k).wait_recv()
            part[m, 4 + k] = (part[m, 4 + k].astype(F32) + got_a[m, k].astype(F32)).astype(BF)
            send_b(m, 2 + k).start()
        product(m, 3)
        return 0

    lax.fori_loop(0, STEPS, step, 0)
    reduce_step(STEPS - 1)
    keep_pre = pltpu.make_async_copy(pv, all_pre.at[yh], loc_sem.at[3])
    keep_pre.start()
    gather(False)
    for m in range(STEPS):
        pre_across(m).wait_recv()
    fix = remote(all_pre.at[1 - yh, :, :, mine], all_pre.at[1 - yh, :, :, mine], fix_sem, (), sibling)
    fix.start()
    finish_step(STEPS - 2)
    finish_step(STEPS - 1)

    def drain(m, _):
        pre_swap(m).wait_send()
        pre_across(m).wait_send()
        for k in range(2):
            send_a(m, k).wait_send()
        for k in range(4):
            send_b(m, k).wait_send()

        @pl.when(section > 0)
        def _():
            send_u(m, 0).wait_send()
            send_u(m, 1).wait_send()

        send_y(m).wait_send()
        grad_own(m).wait()
        grad_other(m).wait()
        return 0

    lax.fori_loop(0, STEPS, drain, 0)
    for index, phase in enumerate(phases):
        for k, c in enumerate(phase()):
            c.wait_send()
            if k >= arrivals[index]:
                c.wait_recv()
    keep_pre.wait()
    fix.wait()


def run_pipeline(weight, acts, gates, out_grad):
    width = weight.shape[0]
    dma = pltpu.SemaphoreType.DMA
    micro = 2 * 256 // STEPS
    return pl.pallas_call(
        pipeline_kernel,
        out_shape=(
            jax.ShapeDtypeStruct((256, 1024), BF),
            jax.ShapeDtypeStruct((4, 4, 2, 256, 1024), BF),
            jax.ShapeDtypeStruct((2, 2, 256, 1024), BF),
        ),
        in_specs=[pl.BlockSpec(memory_space=pl.ANY)] * 4,
        out_specs=(pl.BlockSpec(memory_space=pl.ANY),) * 3,
        scratch_shapes=[
            pltpu.VMEM((8, 512, 1024), BF),
            pltpu.VMEM((2, 256, 512), BF),
            pltpu.VMEM((2, 256, 512), BF),
            pltpu.VMEM((2, micro // 2, 512), BF),
            pltpu.VMEM((2, 256, 1024), BF),
            pltpu.VMEM((STEPS, 8, micro, 512), BF),
            pltpu.VMEM((STEPS, 2, micro, 512), BF),
            pltpu.VMEM((STEPS, 4, micro, 512), BF),
            pltpu.VMEM((STEPS, 2, micro, 512), BF),
            pltpu.VMEM((STEPS, micro, 512), BF),
            pltpu.VMEM((STEPS, micro, 512), BF),
            pltpu.VMEM((2, 256, 512), BF),
            dma((8,)),
            dma((2,)),
            dma((2,)),
            dma((2, STEPS)),
            dma((2, STEPS, 2)),
            dma((2, STEPS, 4)),
            dma((2, STEPS, 2)),
            dma((2, STEPS)),
            dma((2, STEPS)),
            dma((2,)),
            dma((4,)),
            dma((STEPS,)),
            dma((2, STEPS)),
            dma((2, 16)),
            dma((2, 8)),
        ],
        compiler_params=pltpu.CompilerParams(
            collective_id=0, has_side_effects=True, vmem_limit_bytes=40 * 2**20
        ),
        cost_estimate=pl.CostEstimate(
            flops=2 * 512 * 1024 * width // 2, bytes_accessed=2 * width * 1024, transcendentals=0
        ),
        name="pipeline",
    )(weight, acts, gates, out_grad)


def owned_kernel(meta, a0, a1, a2, a3, pre, out):
    i = pl.program_id(0)
    rhs = pre[...].reshape(1024, 1024)
    lhs = jnp.concatenate([a[...].reshape(1024, 128) for a in (a0, a1, a2, a3)], axis=1)
    value = lax.dot_general(lhs, rhs, (((0,), (0,)), ((), ())), preferred_element_type=F32).astype(BF)
    for k in range(4):
        rows = value[k * 128 : (k + 1) * 128]
        out[k * 128 : (k + 1) * 128, :] = jnp.where(4 * i + k < meta[1], rows, jnp.zeros_like(rows))


def run_owned(meta, all_acts, all_pre, cap):
    def place(k):
        def index(i, meta):
            block = jnp.minimum(meta[0] + jnp.minimum(4 * i + k, meta[1] - 1), 63)
            return (0, block // 32, (block // 8) % 4, 0, 0, block % 8)

        return pl.BlockSpec((2, 1, 1, 2, 256, 128), index)

    view = all_acts.reshape(2, 2, 4, 2, 256, 1024)
    return pl.pallas_call(
        owned_kernel,
        out_shape=jax.ShapeDtypeStruct((cap, 1024), BF),
        grid_spec=pltpu.PrefetchScalarGridSpec(
            num_scalar_prefetch=1,
            grid=(cap // 512,),
            in_specs=[place(k) for k in range(4)] + [pl.BlockSpec((2, 2, 256, 1024), lambda i, meta: (0, 0, 0, 0))],
            out_specs=pl.BlockSpec((512, 1024), lambda i, meta: (i, 0)),
        ),
        compiler_params=pltpu.CompilerParams(vmem_limit_bytes=40 * 2**20),
        cost_estimate=pl.CostEstimate(
            flops=2 * cap * 1024 * 1024, bytes_accessed=2 * (2 * cap * 1024 + 1024 * 1024), transcendentals=0
        ),
        name="owned",
    )(meta, view, view, view, view, all_pre)


def on_device(weights, acts, gates, out_grad, owner_rows):
    width = weights.shape[1]
    cap = 3 * width // (2 * lax.axis_size("dp"))
    tokens = acts.shape[1] * acts.shape[2]
    flat = lambda a: a.reshape(tokens, a.shape[-1])
    grads, all_acts, all_pre = run_pipeline(weights[0], flat(acts[0]), flat(gates[0]), flat(out_grad))
    counts = lax.dynamic_index_in_dim(owner_rows, lax.axis_index("section"), 0, keepdims=False)
    owner = lax.axis_index("dp")
    start = jnp.sum(jnp.where(jnp.arange(counts.shape[0]) < owner, counts, 0))
    count = lax.dynamic_index_in_dim(counts, owner, 0, keepdims=False)
    owned = run_owned(jnp.stack([start, count]).astype(jnp.int32), all_acts, all_pre, cap)
    return owned[None, None], grads.reshape(acts.shape)


def solution(mesh):
    placed = (
        P("section", None, "tensor"),
        P("section", None, "dp", "tensor"),
        P("section", None, "dp", "tensor"),
        P(None, "dp", "tensor"),
        P(),
    )
    return jax.shard_map(
        on_device,
        mesh=mesh,
        in_specs=placed,
        out_specs=(P("section", "dp", None, "tensor"), P("section", None, "dp", "tensor")),
        check_vma=False,
    )
```

```python
import jax
import jax.numpy as jnp
from jax import lax
from jax.experimental import pallas as pl
from jax.experimental.pallas import tpu as pltpu
from jax.sharding import PartitionSpec as P

OWN_BLK = 128
BLOCKS = 4
STEPS = 8
MESH = pl.DeviceIdType.MESH
BF = jnp.bfloat16
F32 = jnp.float32


def remote(src, dst, sems, index, device):
    return pltpu.make_async_remote_copy(
        src_ref=src,
        dst_ref=dst,
        send_sem=sems.at[(0,) + index],
        recv_sem=sems.at[(1,) + index],
        device_id=device,
        device_id_type=MESH,
    )


def each(count, body):
    def wrapped(i, _):
        body(i)
        return 0

    lax.fori_loop(0, count, wrapped, 0)


def window_kernel(
    weight, acts, gates, out_grad,
    grads, av, pav,
    own, wv, wt, gv, ov, part, got_a, got_b, got_u, got_y, kept, total, sums,
    w_sem, gate_sem, og_sem, pre_sem, a_sem, b_sem, u_sem, y_sem, ag_sem, fix_sem, loc_sem,
    out_loc_sem, out_sem, back_sem, paced_sem, g_sem, sib_sem,
):
    section = lax.axis_index("section")
    tensor = lax.axis_index("tensor")
    dp = lax.axis_index("dp")
    last_section = lax.axis_size("section") - 1
    x, yl = lax.rem(tensor, 4), tensor // 4
    yh, core = dp // 2, lax.rem(dp, 2)
    y = yh * 2 + yl
    tokens, width = gates.shape
    micro = tokens // STEPS
    half = width // 2
    is_last = section == last_section
    is_first = section == 0

    def at(x_, y_, z_, core_):
        y_ = lax.rem(y_ + 4, 4)
        return (z_, lax.rem(y_, 2) * 4 + lax.rem(x_ + 4, 4), (y_ // 2) * 2 + core_)

    right, left = at(x + 1, y, section, core), at(x - 1, y, section, core)
    up, down = at(x, y + 1, section, core), at(x, y - 1, section, core)
    across = at(x, y + 2, section, core)
    sibling = at(x, y, section, 1 - core)
    other_y = yh * 2 + 1 - yl
    partner = at(x, other_y, section, core)
    diagonal = at(x - 1 + 2 * yl, other_y, section, core)
    below = lax.rem(section + last_section, last_section + 1)
    above = lax.rem(section + 1, last_section + 1)
    below_same, below_other = at(x, y, below, core), at(x, other_y, below, core)
    above_same, above_other = at(x, y, above, core), at(x, other_y, above, core)
    below_sibling, above_sibling = at(x, y, below, 1 - core), at(x, y, above, 1 - core)

    mine = pl.ds(pl.multiple_of(core * half, half), half)
    theirs = pl.ds(pl.multiple_of((1 - core) * half, half), half)

    own_gate = pltpu.make_async_copy(gates.at[:, mine], gv.at[core], loc_sem.at[0])
    own_gate.start()
    own_grad = pltpu.make_async_copy(out_grad.at[:, mine], ov.at[core], loc_sem.at[2])
    pl.when(is_last)(own_grad.start)

    places = (
        (2, 0), (2, 1), (1, 1), (3, 0), (1, 0), (3, 1), (0, 1 - yl), (0, yl),
    )
    loads = []
    for k, (dx, l) in enumerate(places):
        start = (l * 4 + lax.rem(x + dx, 4)) * 1024 + core * half
        load = pltpu.make_async_copy(
            weight.at[pl.ds(pl.multiple_of(start, half), half), :], wv.at[k], w_sem.at[k]
        )
        load.start()
        loads.append(load)
    own_acts = pltpu.make_async_copy(acts, own, loc_sem.at[1])
    keep_own = pltpu.make_async_copy(own, av.at[yh, yl, x, core], loc_sem.at[3])
    own_acts.start()

    barrier = pltpu.get_barrier_semaphore()
    neighbours = (
        right, left, up, down, across, diagonal, sibling, below_same, below_other, below_sibling,
        above_same, above_other, above_sibling,
    )
    for device in neighbours:
        pl.semaphore_signal(barrier, inc=1, device_id=device, device_id_type=MESH)

    def turn(k):
        for j in range(2):
            loads[2 * k + j].wait()
            wt[k, :, j * half : (j + 1) * half] = wv[2 * k + j].T

    turn(0)
    turn(1)
    pl.semaphore_wait(barrier, len(neighbours))

    gate_swap = remote(gates.at[:, theirs], gv.at[core], gate_sem, (), sibling)
    gate_swap.start()
    grad_swap = remote(out_grad.at[:, theirs], ov.at[core], og_sem, (), sibling)
    pl.when(is_last)(grad_swap.start)

    tok = tokens // 2
    lo, hi = pl.ds(0, tok), pl.ds(tok, tok)
    lo_a, lo_b = pl.ds(0, tok // 2), pl.ds(tok // 2, tok // 2)
    hi_a, hi_b = pl.ds(tok, tok // 2), pl.ds(tok + tok // 2, tok // 2)
    xr, xl, x2 = lax.rem(x + 1, 4), lax.rem(x + 3, 4), lax.rem(x + 2, 4)
    yu, yd, y2 = lax.rem(y + 1, 4), lax.rem(y + 3, 4), lax.rem(y + 2, 4)
    piece = tok // STEPS

    def tile(y_, x_, rows=None):
        ref = av.at[y_ // 2, lax.rem(y_, 2), x_, core]
        return ref if rows is None else ref.at[rows]

    def same(k, ref, device):
        return remote(ref, ref, g_sem, (k,), device)

    def sib(k, ref):
        return remote(own if k == 0 else ref, ref, sib_sem, (k,), sibling)

    def paced(which, q, y_lo, x_lo, y_hi, x_hi, to_lo, to_hi):
        rows_lo = pl.ds(pl.multiple_of(q * piece, piece), piece)
        rows_hi = pl.ds(pl.multiple_of(tok + q * piece, piece), piece)
        ref_lo, ref_hi = tile(y_lo, x_lo, rows_lo), tile(y_hi, x_hi, rows_hi)
        src_lo, src_hi = (own.at[rows_lo], own.at[rows_hi]) if which == 0 else (ref_lo, ref_hi)
        return [
            remote(src, ref, paced_sem, (which, q, k), device)
            for k, (src, ref, device) in enumerate(
                [
                    (src_lo, ref_lo, to_lo[0]), (src_lo, ref_lo, to_lo[1]),
                    (src_hi, ref_hi, to_hi[0]), (src_hi, ref_hi, to_hi[1]),
                ]
            )
        ]

    def set_a(q):
        return paced(0, q, y, x, y, x, (right, left), (up, down))

    def set_c(q):
        return paced(1, q, y, xl, yd, x, (up, down), (right, left))

    def set_b():
        return [
            remote(own.at[rows], tile(y, x, rows), g_sem, (k,), device)
            for k, (rows, device) in enumerate([(lo, up), (lo, down), (hi, right), (hi, left)])
        ]

    def set_f():
        return [
            same(4, tile(y, xl, lo_a), right), same(5, tile(y, xr, lo_b), left),
            same(6, tile(yd, x, hi_a), up), same(7, tile(yu, x, hi_b), down),
        ]

    def set_d():
        right_lo, up_hi = tile(y, xr, lo), tile(yu, x, hi)
        return [same(8, right_lo, up), same(9, right_lo, down), same(10, up_hi, right), same(11, up_hi, left)]

    def set_e(q):
        return paced(2, q, y, x2, y2, x, (up, down), (right, left))

    def set_g():
        return [
            same(16, tile(yd, xl, lo_a), up), same(17, tile(yu, xl, lo_b), down),
            same(18, tile(yd, xr, lo_a), up), same(19, tile(yu, xr, lo_b), down),
            same(20, tile(yd, x, lo_a), up), same(21, tile(yu, x, lo_b), down),
            same(22, tile(yd, xl, hi_a), right), same(23, tile(yd, xr, hi_b), left),
            same(24, tile(yu, xl, hi_a), right), same(25, tile(yu, xr, hi_b), left),
            same(26, tile(y, xl, hi_a), right), same(27, tile(y, xr, hi_b), left),
        ]

    def set_h():
        return [
            same(28, tile(yd, x2, lo_a), up), same(29, tile(yu, x2, lo_b), down),
            same(30, tile(y2, xl, hi_a), right), same(31, tile(y2, xr, hi_b), left),
        ]

    tiles = (
        (y, x),
        (y, xl), (y, xr), (yd, x), (yu, x), (yd, xl), (yd, xr), (yu, xl), (yu, xr),
        (y, x2), (y2, x), (yd, x2), (yu, x2), (y2, xl), (y2, xr),
        (y2, x2),
    )

    def sibs(first, end):
        return [sib(k, tile(*tiles[k])) for k in range(first, end)]

    def start(copies):
        for c in copies:
            c.start()

    def arrived(copies):
        for c in copies:
            c.wait_recv()

    def gather_second():
        start(set_f())

    def gather_third():
        each(STEPS, lambda q: start(set_c(q)))
        start(set_d())

    def gather_fourth():
        arrived(set_b())

        @pl.when(section != last_section - 2)
        def _():
            arrived(set_f())
            each(STEPS, lambda q: start(set_e(q)))

        each(STEPS, lambda q: arrived(set_c(q)))
        arrived(set_d())
        start(set_g())
        start(sibs(1, 9))

    def gather_fifth():
        each(STEPS, lambda q: arrived(set_e(q)))
        arrived(set_g())
        start(set_h())
        start(sibs(9, 15))

    def gather_sixth():
        arrived(set_h())
        start(sibs(15, 16))

    turn(2)
    turn(3)
    own_acts.wait()
    keep_own.start()

    @pl.when(section < last_section)
    def _():
        each(STEPS, lambda q: start(set_a(q)))
        start(set_b())
        start(sibs(0, 1))
        each(STEPS, lambda q: arrived(set_a(q)))
        start(set_f())

    @pl.when(section < last_section - 1)
    def _():
        gather_third()

    pl.when(section == last_section - 2)(lambda: arrived(set_f()))
    pl.when(is_first)(gather_fourth)

    own_gate.wait()
    gate_swap.wait()

    @pl.when(is_last)
    def _():
        own_grad.wait()
        grad_swap.wait()

    def rows_of(m):
        return pl.ds(pl.multiple_of(m * micro, micro), micro)

    def pre_swap(m):
        ref = pav.at[yh, :, rows_of(m), mine]
        return remote(ref, ref, pre_sem, (m,), sibling)

    def pre_across(m):
        ref = pav.at[yh, :, rows_of(m), mine]
        return remote(ref, ref, ag_sem, (m,), across)

    def send_a(m, k):
        return remote(part.at[m, k], got_a.at[m, k], a_sem, (m, k), (right, left)[k])

    def send_b(m, k):
        return remote(part.at[m, 2 + k], got_b.at[m, k], b_sem, (m, k), (right, left)[k])

    def send_same(m):
        return remote(part.at[m, 4 + yl], got_b.at[m, 2], b_sem, (m, 2), at(x + 1 - 2 * yl, y, section, core))

    def send_diagonal(m):
        return remote(part.at[m, 5 - yl], got_b.at[m, 3], b_sem, (m, 3), diagonal)

    def send_u(m, k):
        return remote((kept.at[m], part.at[m, 6])[k], got_u.at[m, k], u_sem, (m, k), (below_same, below_other)[k])

    def send_y(m):
        return remote(part.at[m, 6], got_y.at[m], y_sem, (m,), partner)

    def send_back(m, k):
        src = sums.at[(core, 1 - core)[k], rows_of(m), :]
        return remote(src, grads.at[rows_of(m), mine], back_sem, (m, k), (above_same, above_sibling)[k])

    def grad_own(m):
        return pltpu.make_async_copy(total.at[core, rows_of(m), :], grads.at[rows_of(m), mine], out_loc_sem.at[m])

    def grad_other(m):
        return remote(total.at[1 - core, rows_of(m), :], grads.at[rows_of(m), mine], out_sem, (m,), sibling)

    def product(m, k):
        pre = jnp.concatenate([pav[yh, 0, rows_of(m), :], pav[yh, 1, rows_of(m), :]], axis=0)
        value = jnp.dot(pre, wt[k], preferred_element_type=F32).astype(BF)
        part[m, 2 * k] = value[:, :half]
        part[m, 2 * k + 1] = value[:, half:]

    def forward_step(m):
        for k in range(2):
            send_a(m, k).wait_recv()
            part[m, 4 + k] = (part[m, 4 + k].astype(F32) + got_a[m, k].astype(F32)).astype(BF)
        send_diagonal(m).start()
        send_same(m).start()

    def partner_step(m):
        for k in range(2):
            send_b(m, k).wait_recv()
        part[m, 6] = (part[m, 6].astype(F32) + got_b[m, yl].astype(F32)).astype(BF)

        @pl.when(section > 0)
        def _():
            send_u(m, 1).start()

        @pl.when(is_first)
        def _():
            send_y(m).start()

    def reduce_step(m):
        send_same(m).wait_recv()
        send_diagonal(m).wait_recv()
        kept[m] = (
            (part[m, 7].astype(F32) + got_b[m, 1 - yl].astype(F32))
            + (got_b[m, 2].astype(F32) + got_b[m, 3].astype(F32))
        ).astype(BF)

        @pl.when(section > 0)
        def _():
            send_u(m, 0).start()

    def finish_step(m):
        send_y(m).wait_recv()
        value = (kept[m].astype(F32) + got_y[m].astype(F32)).astype(BF)
        total[0, rows_of(m), :] = value[:micro]
        total[1, rows_of(m), :] = value[micro:]
        grad_own(m).start()
        grad_other(m).start()

    def times_gate(m, upstream):
        pre = (upstream.astype(F32) * gv[:, rows_of(m), :].astype(F32)).astype(BF)
        pav[yh, :, rows_of(m), mine] = pre
        pre_swap(m).start()

    def take_step(m):
        @pl.when(is_last)
        def _():
            times_gate(m, ov[:, rows_of(m), :])

        @pl.when(section < last_section)
        def _():
            send_u(m, 0).wait_recv()
            send_u(m, 1).wait_recv()
            value = (got_u[m, 0].astype(F32) + got_u[m, 1].astype(F32)).astype(BF).reshape(2, micro, half)
            times_gate(m, value)
            sums[:, rows_of(m), :] = value

    def give_back(m):
        @pl.when(section < last_section)
        def _():
            for k in range(2):
                send_back(m, k).start()

    def paced_gather(m):
        pl.when(is_last)(lambda: start(set_a(m)))
        pl.when(section == last_section - 1)(lambda: start(set_c(m)))
        pl.when(section == last_section - 2)(lambda: start(set_e(m)))

    def step(m):
        take_step(m)
        pre_across(m).start()
        give_back(m)
        pre_swap(m).wait_recv()
        product(m, 0)
        send_a(m, 0).start()
        send_a(m, 1).start()


        @pl.when(m > 0)
        def _():
            product(m - 1, 2)
            forward_step(m - 1)


        @pl.when(m > 1)
        def _():
            reduce_step(m - 2)


        @pl.when(m > 0)
        def _():
            product(m - 1, 3)

        product(m, 1)
        send_b(m, 0).start()
        send_b(m, 1).start()


        @pl.when(m > 0)
        def _():
            partner_step(m - 1)

        paced_gather(m)


        @pl.when(m > 2)
        def _():
            pl.when(is_first)(lambda: finish_step(m - 3))

        pl.when(is_first & (m == 2))(gather_fifth)
        pl.when(is_first & (m == 4))(gather_sixth)

    fix_ref = pav.at[1 - yh, :, :, mine]
    fix = remote(fix_ref, fix_ref, fix_sem, (), sibling)

    def exchange_pre():
        each(STEPS, lambda m: pre_across(m).wait_recv())
        fix.start()
        fix.wait_recv()

    each(STEPS, step)
    product(STEPS - 1, 2)
    forward_step(STEPS - 1)
    reduce_step(STEPS - 2)
    product(STEPS - 1, 3)
    partner_step(STEPS - 1)

    @pl.when(is_first)
    def _():
        exchange_pre()
        arrived(sibs(0, 16))

    reduce_step(STEPS - 1)

    @pl.when(is_last)
    def _():
        start(set_b())
        start(sibs(0, 1))
        each(STEPS, lambda q: arrived(set_a(q)))
        start(set_f())
        gather_third()

    @pl.when(section == last_section - 1)
    def _():
        start(set_d())

    @pl.when(section > 0)
    def _():
        exchange_pre()
        gather_fourth()
        gather_fifth()
        gather_sixth()
        arrived(sibs(0, 16))

    @pl.when(is_first)
    def _():
        finish_step(STEPS - 3)
        finish_step(STEPS - 2)
        finish_step(STEPS - 1)

    def drain(m):
        pre_swap(m).wait_send()
        pre_across(m).wait_send()
        for k in range(2):
            send_a(m, k).wait_send()
        for k in range(2):
            send_b(m, k).wait_send()
        send_same(m).wait_send()
        send_diagonal(m).wait_send()
        for c in set_a(m) + set_c(m) + set_e(m):
            c.wait_send()

        @pl.when(section > 0)
        def _():
            for k in range(2):
                send_u(m, k).wait_send()
                send_back(m, k).wait_recv()

        @pl.when(section < last_section)
        def _():
            for k in range(2):
                send_back(m, k).wait_send()

        @pl.when(is_first)
        def _():
            send_y(m).wait_send()
            grad_own(m).wait()
            grad_other(m).wait()

    each(STEPS, drain)
    for c in set_b() + set_f() + set_d() + set_g() + set_h() + sibs(0, 16):
        c.wait_send()
    fix.wait_send()
    keep_own.wait()


def run_window(weight, acts, gates, out_grad):
    tokens, width = acts.shape
    rows = weight.shape[0]
    half = width // 2
    dma = pltpu.SemaphoreType.DMA
    micro = 2 * tokens // STEPS
    hbm = pl.BlockSpec(memory_space=pl.ANY)
    return pl.pallas_call(
        window_kernel,
        out_shape=(
            pltpu.VMEM((tokens, width), BF),
            jax.ShapeDtypeStruct((2, 2, 4, 2, tokens, width), BF),
            pltpu.VMEM((2, 2, tokens, width), BF),
        ),
        in_specs=[hbm] * 4,
        out_specs=(pl.BlockSpec(memory_space=pltpu.VMEM), hbm, pl.BlockSpec(memory_space=pltpu.VMEM)),
        scratch_shapes=[
            pltpu.VMEM((tokens, width), BF),
            pltpu.VMEM((8, half, width), BF),
            pltpu.VMEM((4, width, width), BF),
            pltpu.VMEM((2, tokens, half), BF),
            pltpu.VMEM((2, tokens, half), BF),
            pltpu.VMEM((STEPS, 8, micro, half), BF),
            pltpu.VMEM((STEPS, 2, micro, half), BF),
            pltpu.VMEM((STEPS, 4, micro, half), BF),
            pltpu.VMEM((STEPS, 2, micro, half), BF),
            pltpu.VMEM((STEPS, micro, half), BF),
            pltpu.VMEM((STEPS, micro, half), BF),
            pltpu.VMEM((2, tokens, half), BF),
            pltpu.VMEM((2, tokens, half), BF),
            dma((8,)),
            dma((2,)),
            dma((2,)),
            dma((2, STEPS)),
            dma((2, STEPS, 2)),
            dma((2, STEPS, 4)),
            dma((2, STEPS, 2)),
            dma((2, STEPS)),
            dma((2, STEPS)),
            dma((2,)),
            dma((4,)),
            dma((STEPS,)),
            dma((2, STEPS)),
            dma((2, STEPS, 2)),
            dma((2, 3, STEPS, 4)),
            dma((2, 32)),
            dma((2, 16)),
        ],
        compiler_params=pltpu.CompilerParams(
            collective_id=0, has_side_effects=True, vmem_limit_bytes=60 * 2**20
        ),
        cost_estimate=pl.CostEstimate(
            flops=2 * tokens * width * rows,
            bytes_accessed=2 * rows * width,
            transcendentals=0,
        ),
        name="window",
    )(weight, acts, gates, out_grad)


def owned_kernel(owners, acts, pre, owned, held, stage, in_sem, out_sem):
    section, owner = lax.axis_index("section"), lax.axis_index("dp")
    tokens, width = pre.shape[2:]
    first = jnp.int32(0)
    for k in range(3):
        first = first + jnp.where(k < owner, owners[section, k], 0)
    count = owners[section, owner]
    blocks = held.shape[0]
    group = BLOCKS
    rows = group * OWN_BLK

    def load(b):
        block = jnp.clip(first + jnp.minimum(b, count - 1), 0, 63)
        lane = pl.ds(pl.multiple_of(lax.rem(block, 8) * OWN_BLK, OWN_BLK), OWN_BLK)
        src = acts.at[:, lax.div(block, 32), lax.rem(lax.div(block, 8), 4), :, :, lane]
        return pltpu.make_async_copy(src, held.at[b], in_sem.at[b])

    def out(i):
        part = pl.ds(pl.multiple_of(i * rows, rows), rows)
        return pltpu.make_async_copy(stage.at[part], owned.at[part], out_sem.at[i])

    def chunk(i):
        for k in range(group):
            load(group * i + k).wait()
        lhs = jnp.concatenate(
            [held[group * i + k].reshape(4 * tokens, OWN_BLK) for k in range(group)], axis=1
        )
        rhs = pre[...].reshape(4 * tokens, width)
        value = lax.dot_general(lhs, rhs, (((0,), (0,)), ((), ())), preferred_element_type=F32).astype(BF)
        for k in range(group):
            piece = value[k * OWN_BLK : (k + 1) * OWN_BLK]
            stage[pl.ds(pl.multiple_of(i * rows + k * OWN_BLK, OWN_BLK), OWN_BLK), :] = jnp.where(
                group * i + k < count, piece, jnp.zeros_like(piece)
            )
        out(i).start()

    each(blocks, lambda b: load(b).start())
    each(blocks // group, chunk)
    each(blocks // group, lambda i: out(i).wait())


def run_owned(owners, acts, pre, cap):
    tokens, width = pre.shape[2:]
    hbm = pl.BlockSpec(memory_space=pl.ANY)
    blocks = cap // OWN_BLK
    return pl.pallas_call(
        owned_kernel,
        out_shape=jax.ShapeDtypeStruct((cap, width), BF),
        in_specs=[pl.BlockSpec(memory_space=pltpu.SMEM), hbm, pl.BlockSpec(memory_space=pltpu.VMEM)],
        out_specs=hbm,
        scratch_shapes=[
            pltpu.VMEM((blocks, 2, 2, tokens, OWN_BLK), BF),
            pltpu.VMEM((cap, width), BF),
            pltpu.SemaphoreType.DMA((blocks,)),
            pltpu.SemaphoreType.DMA((blocks // BLOCKS,)),
        ],
        compiler_params=pltpu.CompilerParams(vmem_limit_bytes=40 * 2**20),
        cost_estimate=pl.CostEstimate(
            flops=8 * cap * width * tokens, bytes_accessed=12 * cap * width, transcendentals=0
        ),
        name="owned",
    )(owners, acts, pre)


def on_device(weights, acts, gates, out_grad, owner_rows):
    width = weights.shape[1]
    cap = 3 * width // (2 * lax.axis_size("dp"))
    tokens = acts.shape[1] * acts.shape[2]

    def flat(a):
        return a.reshape(tokens, a.shape[-1])

    grads, av, pav = run_window(weights[0], flat(acts[0]), flat(gates[0]), flat(out_grad))
    owned = run_owned(owner_rows, av, pav, cap)
    return owned[None, None], grads.reshape(acts.shape)


def solution(mesh):
    placed = (
        P("section", None, "tensor"),
        P("section", None, "dp", "tensor"),
        P("section", None, "dp", "tensor"),
        P(None, "dp", "tensor"),
        P(),
    )
    return jax.shard_map(
        on_device,
        mesh=mesh,
        in_specs=placed,
        out_specs=(P("section", "dp", None, "tensor"), P("section", None, "dp", "tensor")),
        check_vma=False,
    )
```

```python
import jax
import jax.numpy as jnp
from jax import lax
from jax.experimental import pallas as pl
from jax.experimental.pallas import tpu as pltpu
from jax.sharding import PartitionSpec as P

OWN_BLK = 128
BLOCKS = 4
STEPS = 8
MESH = pl.DeviceIdType.MESH
BF = jnp.bfloat16
F32 = jnp.float32


def remote(src, dst, sems, index, device):
    return pltpu.make_async_remote_copy(
        src_ref=src,
        dst_ref=dst,
        send_sem=sems.at[(0,) + index],
        recv_sem=sems.at[(1,) + index],
        device_id=device,
        device_id_type=MESH,
    )


def each(count, body):
    def wrapped(i, _):
        body(i)
        return 0

    lax.fori_loop(0, count, wrapped, 0)


def window_kernel(
    weight, acts, gates, out_grad,
    grads, av, pav,
    own, wv, wt, gv, ov, part, got_a, got_b, got_u, got_y, kept, total, sums,
    w_sem, gate_sem, og_sem, pre_sem, a_sem, b_sem, u_sem, y_sem, ag_sem, fix_sem, loc_sem,
    out_loc_sem, out_sem, back_sem, paced_sem, g_sem, sib_sem,
):
    section = lax.axis_index("section")
    tensor = lax.axis_index("tensor")
    dp = lax.axis_index("dp")
    last_section = lax.axis_size("section") - 1
    x, yl = lax.rem(tensor, 4), tensor // 4
    yh, core = dp // 2, lax.rem(dp, 2)
    y = yh * 2 + yl
    tokens, width = gates.shape
    micro = tokens // STEPS
    half = width // 2
    is_last = section == last_section
    is_first = section == 0

    def at(x_, y_, z_, core_):
        y_ = lax.rem(y_ + 4, 4)
        return (z_, lax.rem(y_, 2) * 4 + lax.rem(x_ + 4, 4), (y_ // 2) * 2 + core_)

    right, left = at(x + 1, y, section, core), at(x - 1, y, section, core)
    up, down = at(x, y + 1, section, core), at(x, y - 1, section, core)
    across = at(x, y + 2, section, core)
    sibling = at(x, y, section, 1 - core)
    other_y = yh * 2 + 1 - yl
    partner = at(x, other_y, section, core)
    diagonal = at(x - 1 + 2 * yl, other_y, section, core)
    below = lax.rem(section + last_section, last_section + 1)
    above = lax.rem(section + 1, last_section + 1)
    below_same, below_other = at(x, y, below, core), at(x, other_y, below, core)
    above_same, above_other = at(x, y, above, core), at(x, other_y, above, core)
    below_sibling, above_sibling = at(x, y, below, 1 - core), at(x, y, above, 1 - core)

    mine = pl.ds(pl.multiple_of(core * half, half), half)
    theirs = pl.ds(pl.multiple_of((1 - core) * half, half), half)

    own_gate = pltpu.make_async_copy(gates.at[:, mine], gv.at[core], loc_sem.at[0])
    own_gate.start()
    own_grad = pltpu.make_async_copy(out_grad.at[:, mine], ov.at[core], loc_sem.at[2])
    pl.when(is_last)(own_grad.start)

    places = (
        (2, 0), (2, 1), (1, 1), (3, 0), (1, 0), (3, 1), (0, 1 - yl), (0, yl),
    )
    loads = []
    for k, (dx, l) in enumerate(places):
        start = (l * 4 + lax.rem(x + dx, 4)) * 1024 + core * half
        load = pltpu.make_async_copy(
            weight.at[pl.ds(pl.multiple_of(start, half), half), :], wv.at[k], w_sem.at[k]
        )
        load.start()
        loads.append(load)
    own_acts = pltpu.make_async_copy(acts, own, loc_sem.at[1])
    keep_own = pltpu.make_async_copy(own, av.at[yh, yl, x, core], loc_sem.at[3])
    own_acts.start()

    barrier = pltpu.get_barrier_semaphore()
    neighbours = (
        right, left, up, down, across, diagonal, sibling, below_same, below_other, below_sibling,
        above_same, above_other, above_sibling,
    )
    for device in neighbours:
        pl.semaphore_signal(barrier, inc=1, device_id=device, device_id_type=MESH)

    def turn(k):
        for j in range(2):
            loads[2 * k + j].wait()
            wt[k, :, j * half : (j + 1) * half] = wv[2 * k + j].T

    turn(0)
    pl.semaphore_wait(barrier, len(neighbours))

    gate_swap = remote(gates.at[:, theirs], gv.at[core], gate_sem, (), sibling)
    gate_swap.start()
    grad_swap = remote(out_grad.at[:, theirs], ov.at[core], og_sem, (), sibling)
    pl.when(is_last)(grad_swap.start)

    tok = tokens // 2
    lo, hi = pl.ds(0, tok), pl.ds(tok, tok)
    lo_a, lo_b = pl.ds(0, tok // 2), pl.ds(tok // 2, tok // 2)
    hi_a, hi_b = pl.ds(tok, tok // 2), pl.ds(tok + tok // 2, tok // 2)
    xr, xl, x2 = lax.rem(x + 1, 4), lax.rem(x + 3, 4), lax.rem(x + 2, 4)
    yu, yd, y2 = lax.rem(y + 1, 4), lax.rem(y + 3, 4), lax.rem(y + 2, 4)
    piece = tok // STEPS

    def tile(y_, x_, rows=None):
        ref = av.at[y_ // 2, lax.rem(y_, 2), x_, core]
        return ref if rows is None else ref.at[rows]

    def same(k, ref, device):
        return remote(ref, ref, g_sem, (k,), device)

    def sib(k, ref):
        return remote(own if k == 0 else ref, ref, sib_sem, (k,), sibling)

    def paced(which, q, y_lo, x_lo, y_hi, x_hi, to_lo, to_hi):
        rows_lo = pl.ds(pl.multiple_of(q * piece, piece), piece)
        rows_hi = pl.ds(pl.multiple_of(tok + q * piece, piece), piece)
        ref_lo, ref_hi = tile(y_lo, x_lo, rows_lo), tile(y_hi, x_hi, rows_hi)
        src_lo, src_hi = (own.at[rows_lo], own.at[rows_hi]) if which == 0 else (ref_lo, ref_hi)
        return [
            remote(src, ref, paced_sem, (which, q, k), device)
            for k, (src, ref, device) in enumerate(
                [
                    (src_lo, ref_lo, to_lo[0]), (src_lo, ref_lo, to_lo[1]),
                    (src_hi, ref_hi, to_hi[0]), (src_hi, ref_hi, to_hi[1]),
                ]
            )
        ]

    def set_a(q):
        return paced(0, q, y, x, y, x, (right, left), (up, down))

    def set_c(q):
        return paced(1, q, y, xl, yd, x, (up, down), (right, left))

    def set_b():
        return [
            remote(own.at[rows], tile(y, x, rows), g_sem, (k,), device)
            for k, (rows, device) in enumerate([(lo, up), (lo, down), (hi, right), (hi, left)])
        ]

    def set_f():
        return [
            same(4, tile(y, xl, lo_a), right), same(5, tile(y, xr, lo_b), left),
            same(6, tile(yd, x, hi_a), up), same(7, tile(yu, x, hi_b), down),
        ]

    def set_d():
        right_lo, up_hi = tile(y, xr, lo), tile(yu, x, hi)
        return [same(8, right_lo, up), same(9, right_lo, down), same(10, up_hi, right), same(11, up_hi, left)]

    def set_e(q):
        return paced(2, q, y, x2, y2, x, (up, down), (right, left))

    def set_g():
        return [
            same(16, tile(yd, xl, lo_a), up), same(17, tile(yu, xl, lo_b), down),
            same(18, tile(yd, xr, lo_a), up), same(19, tile(yu, xr, lo_b), down),
            same(20, tile(yd, x, lo_a), up), same(21, tile(yu, x, lo_b), down),
            same(22, tile(yd, xl, hi_a), right), same(23, tile(yd, xr, hi_b), left),
            same(24, tile(yu, xl, hi_a), right), same(25, tile(yu, xr, hi_b), left),
            same(26, tile(y, xl, hi_a), right), same(27, tile(y, xr, hi_b), left),
        ]

    def set_h():
        return [
            same(28, tile(yd, x2, lo_a), up), same(29, tile(yu, x2, lo_b), down),
            same(30, tile(y2, xl, hi_a), right), same(31, tile(y2, xr, hi_b), left),
        ]

    tiles = (
        (y, x),
        (y, xl), (y, xr), (yd, x), (yu, x), (yd, xl), (yd, xr), (yu, xl), (yu, xr),
        (y, x2), (y2, x), (yd, x2), (yu, x2), (y2, xl), (y2, xr),
        (y2, x2),
    )

    def owned_there(k, core_):
        y_, x_ = tiles[k]
        t = lax.rem(y_, 2) * 4 + x_
        owner = 2 * yh + core_
        lowest = jnp.where(owner == 0, 0, jnp.where(owner == 1, 1, jnp.where(owner == 2, 2, 5)))
        highest = jnp.where(owner == 0, 1, jnp.where(owner == 1, 4, jnp.where(owner == 2, 6, 7)))
        return (t >= lowest) & (t <= highest)

    def start_sibs(first, end):
        for k in range(first, end):
            pl.when(owned_there(k, 1 - core))(sib(k, tile(*tiles[k])).start)

    def arrived_sibs():
        for k in range(16):
            pl.when(owned_there(k, core))(sib(k, tile(*tiles[k])).wait_recv)

    def sent_sibs():
        for k in range(16):
            pl.when(owned_there(k, 1 - core))(sib(k, tile(*tiles[k])).wait_send)

    def start(copies):
        for c in copies:
            c.start()

    def arrived(copies):
        for c in copies:
            c.wait_recv()

    def gather_second():
        start(set_f())

    def gather_third():
        each(STEPS, lambda q: start(set_c(q)))
        start(set_d())

    def gather_fourth():
        arrived(set_b())

        @pl.when(section != last_section - 2)
        def _():
            arrived(set_f())
            each(STEPS, lambda q: start(set_e(q)))

        each(STEPS, lambda q: arrived(set_c(q)))
        arrived(set_d())
        start(set_g())
        start_sibs(1, 9)

    def gather_fifth():
        each(STEPS, lambda q: arrived(set_e(q)))
        arrived(set_g())
        start(set_h())
        start_sibs(9, 15)

    def gather_sixth():
        arrived(set_h())
        start_sibs(15, 16)

    turn(1)
    own_acts.wait()
    keep_own.start()

    @pl.when(section < last_section)
    def _():
        each(STEPS, lambda q: start(set_a(q)))
        start(set_b())
        start_sibs(0, 1)
        each(STEPS, lambda q: arrived(set_a(q)))
        start(set_f())

    @pl.when(section < last_section - 1)
    def _():
        gather_third()

    @pl.when(section == last_section - 2)
    def _():
        arrived(set_f())
        each(STEPS, lambda q: start(set_e(q)))

    @pl.when(is_first)
    def _():
        gather_fourth()
        gather_fifth()


    @pl.when(section < last_section)
    def _():
        turn(2)
        turn(3)

    own_gate.wait()
    gate_swap.wait()

    @pl.when(is_last)
    def _():
        own_grad.wait()
        grad_swap.wait()

    def rows_of(m):
        return pl.ds(pl.multiple_of(m * micro, micro), micro)

    def pre_swap(m):
        ref = pav.at[yh, :, rows_of(m), mine]
        return remote(ref, ref, pre_sem, (m,), sibling)

    def pre_across(m):
        ref = pav.at[yh, :, rows_of(m), mine]
        return remote(ref, ref, ag_sem, (m,), across)

    def send_a(m, k):
        return remote(part.at[m, k], got_a.at[m, k], a_sem, (m, k), (right, left)[k])

    def send_b(m, k):
        return remote(part.at[m, 2 + k], got_b.at[m, k], b_sem, (m, k), (right, left)[k])

    def send_same(m):
        return remote(part.at[m, 4 + yl], got_b.at[m, 2], b_sem, (m, 2), at(x + 1 - 2 * yl, y, section, core))

    def send_diagonal(m):
        return remote(part.at[m, 5 - yl], got_b.at[m, 3], b_sem, (m, 3), diagonal)

    def send_u(m, k):
        return remote((kept.at[m], part.at[m, 6])[k], got_u.at[m, k], u_sem, (m, k), (below_same, below_other)[k])

    def send_y(m):
        return remote(part.at[m, 6], got_y.at[m], y_sem, (m,), partner)

    def send_back(m, k):
        src = sums.at[(core, 1 - core)[k], rows_of(m), :]
        return remote(src, grads.at[rows_of(m), mine], back_sem, (m, k), (above_same, above_sibling)[k])

    def grad_own(m):
        return pltpu.make_async_copy(total.at[core, rows_of(m), :], grads.at[rows_of(m), mine], out_loc_sem.at[m])

    def grad_other(m):
        return remote(total.at[1 - core, rows_of(m), :], grads.at[rows_of(m), mine], out_sem, (m,), sibling)

    def product(m, k):
        pre = jnp.concatenate([pav[yh, 0, rows_of(m), :], pav[yh, 1, rows_of(m), :]], axis=0)
        value = jnp.dot(pre, wt[k], preferred_element_type=F32).astype(BF)
        part[m, 2 * k] = value[:, :half]
        part[m, 2 * k + 1] = value[:, half:]

    def forward_step(m):
        for k in range(2):
            send_a(m, k).wait_recv()
            part[m, 4 + k] = (part[m, 4 + k].astype(F32) + got_a[m, k].astype(F32)).astype(BF)
        send_diagonal(m).start()
        send_same(m).start()

    def partner_step(m):
        for k in range(2):
            send_b(m, k).wait_recv()
        part[m, 6] = (part[m, 6].astype(F32) + got_b[m, yl].astype(F32)).astype(BF)

        @pl.when(section > 0)
        def _():
            send_u(m, 1).start()

        @pl.when(is_first)
        def _():
            send_y(m).start()

    def reduce_step(m):
        send_same(m).wait_recv()
        send_diagonal(m).wait_recv()
        kept[m] = (
            (part[m, 7].astype(F32) + got_b[m, 1 - yl].astype(F32))
            + (got_b[m, 2].astype(F32) + got_b[m, 3].astype(F32))
        ).astype(BF)

        @pl.when(section > 0)
        def _():
            send_u(m, 0).start()

    def finish_step(m):
        send_y(m).wait_recv()
        value = (kept[m].astype(F32) + got_y[m].astype(F32)).astype(BF)
        total[0, rows_of(m), :] = value[:micro]
        total[1, rows_of(m), :] = value[micro:]
        grad_own(m).start()
        grad_other(m).start()

    def times_gate(m, upstream):
        pre = (upstream.astype(F32) * gv[:, rows_of(m), :].astype(F32)).astype(BF)
        pav[yh, :, rows_of(m), mine] = pre
        pre_swap(m).start()

    def take_step(m):
        @pl.when(is_last)
        def _():
            times_gate(m, ov[:, rows_of(m), :])

        @pl.when(section < last_section)
        def _():
            send_u(m, 0).wait_recv()
            send_u(m, 1).wait_recv()
            value = (got_u[m, 0].astype(F32) + got_u[m, 1].astype(F32)).astype(BF).reshape(2, micro, half)
            times_gate(m, value)
            sums[:, rows_of(m), :] = value

    def give_back(m):
        @pl.when(section < last_section)
        def _():
            for k in range(2):
                send_back(m, k).start()

    def step(m):
        take_step(m)
        pre_across(m).start()
        give_back(m)
        pre_swap(m).wait_recv()
        product(m, 0)
        send_a(m, 0).start()
        send_a(m, 1).start()


        @pl.when(m > 0)
        def _():
            product(m - 1, 2)
            forward_step(m - 1)


        @pl.when(m > 1)
        def _():
            reduce_step(m - 2)


        @pl.when(m > 0)
        def _():
            product(m - 1, 3)

        product(m, 1)
        send_b(m, 0).start()
        send_b(m, 1).start()


        @pl.when(m > 0)
        def _():
            partner_step(m - 1)


        @pl.when(m > 2)
        def _():
            pl.when(is_first)(lambda: finish_step(m - 3))

        pl.when(is_first & (m == 2))(gather_sixth)

        @pl.when(is_last & (m == 0))
        def _():
            turn(2)
            turn(3)


    fix_ref = pav.at[1 - yh, :, :, mine]
    fix = remote(fix_ref, fix_ref, fix_sem, (), sibling)

    def exchange_pre():
        each(STEPS, lambda m: pre_across(m).wait_recv())
        fix.start()
        fix.wait_recv()

    each(STEPS, step)
    product(STEPS - 1, 2)
    forward_step(STEPS - 1)
    reduce_step(STEPS - 2)
    product(STEPS - 1, 3)
    partner_step(STEPS - 1)

    @pl.when(is_first)
    def _():
        exchange_pre()
        arrived_sibs()

    reduce_step(STEPS - 1)

    @pl.when(is_last)
    def _():
        each(STEPS, lambda q: start(set_a(q)))
        start(set_b())
        start_sibs(0, 1)
        each(STEPS, lambda q: arrived(set_a(q)))
        start(set_f())
        gather_third()

    @pl.when(section == last_section - 1)
    def _():
        gather_third()

    @pl.when(section > 0)
    def _():
        exchange_pre()
        gather_fourth()
        gather_fifth()
        gather_sixth()
        arrived_sibs()

    @pl.when(is_first)
    def _():
        finish_step(STEPS - 3)
        finish_step(STEPS - 2)
        finish_step(STEPS - 1)

    def drain(m):
        pre_swap(m).wait_send()
        pre_across(m).wait_send()
        for k in range(2):
            send_a(m, k).wait_send()
        for k in range(2):
            send_b(m, k).wait_send()
        send_same(m).wait_send()
        send_diagonal(m).wait_send()
        for c in set_a(m) + set_c(m) + set_e(m):
            c.wait_send()

        @pl.when(section > 0)
        def _():
            for k in range(2):
                send_u(m, k).wait_send()
                send_back(m, k).wait_recv()

        @pl.when(section < last_section)
        def _():
            for k in range(2):
                send_back(m, k).wait_send()

        @pl.when(is_first)
        def _():
            send_y(m).wait_send()
            grad_own(m).wait()
            grad_other(m).wait()

    each(STEPS, drain)
    for c in set_b() + set_f() + set_d() + set_g() + set_h():
        c.wait_send()
    sent_sibs()
    fix.wait_send()
    keep_own.wait()


def run_window(weight, acts, gates, out_grad):
    tokens, width = acts.shape
    rows = weight.shape[0]
    half = width // 2
    dma = pltpu.SemaphoreType.DMA
    micro = 2 * tokens // STEPS
    hbm = pl.BlockSpec(memory_space=pl.ANY)
    return pl.pallas_call(
        window_kernel,
        out_shape=(
            pltpu.VMEM((tokens, width), BF),
            jax.ShapeDtypeStruct((2, 2, 4, 2, tokens, width), BF),
            pltpu.VMEM((2, 2, tokens, width), BF),
        ),
        in_specs=[hbm] * 4,
        out_specs=(pl.BlockSpec(memory_space=pltpu.VMEM), hbm, pl.BlockSpec(memory_space=pltpu.VMEM)),
        scratch_shapes=[
            pltpu.VMEM((tokens, width), BF),
            pltpu.VMEM((8, half, width), BF),
            pltpu.VMEM((4, width, width), BF),
            pltpu.VMEM((2, tokens, half), BF),
            pltpu.VMEM((2, tokens, half), BF),
            pltpu.VMEM((STEPS, 8, micro, half), BF),
            pltpu.VMEM((STEPS, 2, micro, half), BF),
            pltpu.VMEM((STEPS, 4, micro, half), BF),
            pltpu.VMEM((STEPS, 2, micro, half), BF),
            pltpu.VMEM((STEPS, micro, half), BF),
            pltpu.VMEM((STEPS, micro, half), BF),
            pltpu.VMEM((2, tokens, half), BF),
            pltpu.VMEM((2, tokens, half), BF),
            dma((8,)),
            dma((2,)),
            dma((2,)),
            dma((2, STEPS)),
            dma((2, STEPS, 2)),
            dma((2, STEPS, 4)),
            dma((2, STEPS, 2)),
            dma((2, STEPS)),
            dma((2, STEPS)),
            dma((2,)),
            dma((4,)),
            dma((STEPS,)),
            dma((2, STEPS)),
            dma((2, STEPS, 2)),
            dma((2, 3, STEPS, 4)),
            dma((2, 32)),
            dma((2, 16)),
        ],
        compiler_params=pltpu.CompilerParams(
            collective_id=0, has_side_effects=True, vmem_limit_bytes=60 * 2**20
        ),
        cost_estimate=pl.CostEstimate(
            flops=2 * tokens * width * rows,
            bytes_accessed=2 * rows * width,
            transcendentals=0,
        ),
        name="window",
    )(weight, acts, gates, out_grad)


def owned_kernel(owners, acts, pre, grads, owned, grads_out, held, stage, in_sem, out_sem, copy_sem):
    section, owner = lax.axis_index("section"), lax.axis_index("dp")
    tokens, width = pre.shape[2:]
    first = jnp.int32(0)
    for k in range(3):
        first = first + jnp.where(k < owner, owners[section, k], 0)
    count = owners[section, owner]
    blocks = held.shape[0]
    group = BLOCKS
    rows = group * OWN_BLK

    def load(b):
        block = jnp.clip(first + jnp.minimum(b, count - 1), 0, 63)
        lane = pl.ds(pl.multiple_of(lax.rem(block, 8) * OWN_BLK, OWN_BLK), OWN_BLK)
        src = acts.at[:, lax.div(block, 32), lax.rem(lax.div(block, 8), 4), :, :, lane]
        return pltpu.make_async_copy(src, held.at[b], in_sem.at[b])

    def out(i):
        part = pl.ds(pl.multiple_of(i * rows, rows), rows)
        return pltpu.make_async_copy(stage.at[part], owned.at[part], out_sem.at[i])

    def chunk(i):
        for k in range(group):
            load(group * i + k).wait()
        lhs = jnp.concatenate(
            [held[group * i + k].reshape(4 * tokens, OWN_BLK) for k in range(group)], axis=1
        )
        rhs = pre[...].reshape(4 * tokens, width)
        value = lax.dot_general(lhs, rhs, (((0,), (0,)), ((), ())), preferred_element_type=F32).astype(BF)
        for k in range(group):
            piece = value[k * OWN_BLK : (k + 1) * OWN_BLK]
            stage[pl.ds(pl.multiple_of(i * rows + k * OWN_BLK, OWN_BLK), OWN_BLK), :] = jnp.where(
                group * i + k < count, piece, jnp.zeros_like(piece)
            )
        out(i).start()

    each(blocks, lambda b: load(b).start())
    keep = pltpu.make_async_copy(grads, grads_out, copy_sem)
    keep.start()
    each(blocks // group, chunk)
    each(blocks // group, lambda i: out(i).wait())
    keep.wait()


def run_owned(owners, acts, pre, grads, cap):
    tokens, width = pre.shape[2:]
    hbm = pl.BlockSpec(memory_space=pl.ANY)
    blocks = cap // OWN_BLK
    return pl.pallas_call(
        owned_kernel,
        out_shape=(jax.ShapeDtypeStruct((cap, width), BF), jax.ShapeDtypeStruct(grads.shape, BF)),
        in_specs=[pl.BlockSpec(memory_space=pltpu.SMEM), hbm] + [pl.BlockSpec(memory_space=pltpu.VMEM)] * 2,
        out_specs=(hbm, hbm),
        scratch_shapes=[
            pltpu.VMEM((blocks, 2, 2, tokens, OWN_BLK), BF),
            pltpu.VMEM((cap, width), BF),
            pltpu.SemaphoreType.DMA((blocks,)),
            pltpu.SemaphoreType.DMA((blocks // BLOCKS,)),
            pltpu.SemaphoreType.DMA,
        ],
        compiler_params=pltpu.CompilerParams(vmem_limit_bytes=40 * 2**20),
        cost_estimate=pl.CostEstimate(
            flops=8 * cap * width * tokens, bytes_accessed=12 * cap * width, transcendentals=0
        ),
        name="owned",
    )(owners, acts, pre, grads)


def on_device(weights, acts, gates, out_grad, owner_rows):
    width = weights.shape[1]
    cap = 3 * width // (2 * lax.axis_size("dp"))
    tokens = acts.shape[1] * acts.shape[2]

    def flat(a):
        return a.reshape(tokens, a.shape[-1])

    grads, av, pav = run_window(weights[0], flat(acts[0]), flat(gates[0]), flat(out_grad))
    owned, grads = run_owned(owner_rows, av, pav, grads, cap)
    return owned[None, None], grads.reshape(acts.shape)


def solution(mesh):
    placed = (
        P("section", None, "tensor"),
        P("section", None, "dp", "tensor"),
        P("section", None, "dp", "tensor"),
        P(None, "dp", "tensor"),
        P(),
    )
    return jax.shard_map(
        on_device,
        mesh=mesh,
        in_specs=placed,
        out_specs=(P("section", "dp", None, "tensor"), P("section", None, "dp", "tensor")),
        check_vma=False,
    )
```

```python
import jax
import jax.numpy as jnp
from jax import lax
from jax.experimental import pallas as pl
from jax.experimental.pallas import tpu as pltpu
from jax.sharding import PartitionSpec as P

OWN_BLK = 128
BLOCKS = 4
STEPS = 8
MESH = pl.DeviceIdType.MESH
BF = jnp.bfloat16
F32 = jnp.float32


def remote(src, dst, sems, index, device):
    return pltpu.make_async_remote_copy(
        src_ref=src,
        dst_ref=dst,
        send_sem=sems.at[(0,) + index],
        recv_sem=sems.at[(1,) + index],
        device_id=device,
        device_id_type=MESH,
    )


def each(count, body):
    def wrapped(i, _):
        body(i)
        return 0

    lax.fori_loop(0, count, wrapped, 0)


def window_kernel(
    weight, acts, gates, out_grad,
    grads, av, pav,
    own, wv, wt, gv, ov, part, got_a, got_b, got_u, got_y, kept, total, sums,
    w_sem, gate_sem, og_sem, pre_sem, a_sem, b_sem, u_sem, y_sem, ag_sem, fix_sem, loc_sem,
    out_loc_sem, out_sem, back_sem, paced_sem, g_sem, sib_sem,
):
    section = lax.axis_index("section")
    tensor = lax.axis_index("tensor")
    dp = lax.axis_index("dp")
    last_section = lax.axis_size("section") - 1
    x, yl = lax.rem(tensor, 4), tensor // 4
    yh, core = dp // 2, lax.rem(dp, 2)
    y = yh * 2 + yl
    tokens, width = gates.shape
    micro = tokens // STEPS
    half = width // 2
    is_last = section == last_section
    is_first = section == 0

    def at(x_, y_, z_, core_):
        y_ = lax.rem(y_ + 4, 4)
        return (z_, lax.rem(y_, 2) * 4 + lax.rem(x_ + 4, 4), (y_ // 2) * 2 + core_)

    right, left = at(x + 1, y, section, core), at(x - 1, y, section, core)
    up, down = at(x, y + 1, section, core), at(x, y - 1, section, core)
    across = at(x, y + 2, section, core)
    sibling = at(x, y, section, 1 - core)
    other_y = yh * 2 + 1 - yl
    partner = at(x, other_y, section, core)
    diagonal = at(x - 1 + 2 * yl, other_y, section, core)
    below = lax.rem(section + last_section, last_section + 1)
    above = lax.rem(section + 1, last_section + 1)
    below_same, below_other = at(x, y, below, core), at(x, other_y, below, core)
    above_same, above_other = at(x, y, above, core), at(x, other_y, above, core)
    below_sibling, above_sibling = at(x, y, below, 1 - core), at(x, y, above, 1 - core)

    mine = pl.ds(pl.multiple_of(core * half, half), half)
    theirs = pl.ds(pl.multiple_of((1 - core) * half, half), half)

    own_gate = pltpu.make_async_copy(gates.at[:, mine], gv.at[core], loc_sem.at[0])
    own_gate.start()
    own_grad = pltpu.make_async_copy(out_grad.at[:, mine], ov.at[core], loc_sem.at[2])
    pl.when(is_last)(own_grad.start)

    places = (
        (2, 0), (2, 1), (1, 1), (3, 0), (1, 0), (3, 1), (0, 1 - yl), (0, yl),
    )
    loads = []
    for k, (dx, l) in enumerate(places):
        start = (l * 4 + lax.rem(x + dx, 4)) * 1024 + core * half
        load = pltpu.make_async_copy(
            weight.at[pl.ds(pl.multiple_of(start, half), half), :], wv.at[k], w_sem.at[k]
        )
        load.start()
        loads.append(load)
    own_acts = pltpu.make_async_copy(acts, own, loc_sem.at[1])
    keep_own = pltpu.make_async_copy(own, av.at[yh, yl, x, core], loc_sem.at[3])
    own_acts.start()

    barrier = pltpu.get_barrier_semaphore()
    neighbours = (
        right, left, up, down, across, diagonal, sibling, below_same, below_other, below_sibling,
        above_same, above_other, above_sibling,
    )
    for device in neighbours:
        pl.semaphore_signal(barrier, inc=1, device_id=device, device_id_type=MESH)

    def turn(k):
        for j in range(2):
            loads[2 * k + j].wait()
            wt[k, :, j * half : (j + 1) * half] = wv[2 * k + j].T

    turn(0)
    pl.semaphore_wait(barrier, len(neighbours))

    first_rows, later_rows = pl.ds(0, micro), pl.ds(micro, tokens - micro)

    def swap(src, dst, sems, k, rows):
        return remote(src.at[rows, theirs], dst.at[core, rows], sems, (k,), sibling)

    gate_swaps = [swap(gates, gv, gate_sem, k, rows) for k, rows in enumerate((first_rows, later_rows))]
    grad_swaps = [swap(out_grad, ov, og_sem, k, rows) for k, rows in enumerate((first_rows, later_rows))]
    gate_swaps[0].start()
    pl.when(is_last)(grad_swaps[0].start)
    gate_swaps[1].start()
    pl.when(is_last)(grad_swaps[1].start)

    tok = tokens // 2
    lo, hi = pl.ds(0, tok), pl.ds(tok, tok)
    lo_a, lo_b = pl.ds(0, tok // 2), pl.ds(tok // 2, tok // 2)
    hi_a, hi_b = pl.ds(tok, tok // 2), pl.ds(tok + tok // 2, tok // 2)
    xr, xl, x2 = lax.rem(x + 1, 4), lax.rem(x + 3, 4), lax.rem(x + 2, 4)
    yu, yd, y2 = lax.rem(y + 1, 4), lax.rem(y + 3, 4), lax.rem(y + 2, 4)
    piece = tok // STEPS

    def tile(y_, x_, rows=None):
        ref = av.at[y_ // 2, lax.rem(y_, 2), x_, core]
        return ref if rows is None else ref.at[rows]

    def same(k, ref, device):
        return remote(ref, ref, g_sem, (k,), device)

    def sib(k, ref):
        return remote(own if k == 0 else ref, ref, sib_sem, (k,), sibling)

    def paced(which, q, y_lo, x_lo, y_hi, x_hi, to_lo, to_hi):
        rows_lo = pl.ds(pl.multiple_of(q * piece, piece), piece)
        rows_hi = pl.ds(pl.multiple_of(tok + q * piece, piece), piece)
        ref_lo, ref_hi = tile(y_lo, x_lo, rows_lo), tile(y_hi, x_hi, rows_hi)
        src_lo, src_hi = (own.at[rows_lo], own.at[rows_hi]) if which == 0 else (ref_lo, ref_hi)
        return [
            remote(src, ref, paced_sem, (which, q, k), device)
            for k, (src, ref, device) in enumerate(
                [
                    (src_lo, ref_lo, to_lo[0]), (src_lo, ref_lo, to_lo[1]),
                    (src_hi, ref_hi, to_hi[0]), (src_hi, ref_hi, to_hi[1]),
                ]
            )
        ]

    def set_a(q):
        return paced(0, q, y, x, y, x, (right, left), (up, down))

    def set_c(q):
        return paced(1, q, y, xl, yd, x, (up, down), (right, left))

    def set_b():
        return [
            remote(own.at[rows], tile(y, x, rows), g_sem, (k,), device)
            for k, (rows, device) in enumerate([(lo, up), (lo, down), (hi, right), (hi, left)])
        ]

    def set_f():
        return [
            same(4, tile(y, xl, lo_a), right), same(5, tile(y, xr, lo_b), left),
            same(6, tile(yd, x, hi_a), up), same(7, tile(yu, x, hi_b), down),
        ]

    def set_d():
        right_lo, up_hi = tile(y, xr, lo), tile(yu, x, hi)
        return [same(8, right_lo, up), same(9, right_lo, down), same(10, up_hi, right), same(11, up_hi, left)]

    def set_e(q):
        return paced(2, q, y, x2, y2, x, (up, down), (right, left))

    def set_g():
        return [
            same(16, tile(yd, xl, lo_a), up), same(17, tile(yu, xl, lo_b), down),
            same(18, tile(yd, xr, lo_a), up), same(19, tile(yu, xr, lo_b), down),
            same(20, tile(yd, x, lo_a), up), same(21, tile(yu, x, lo_b), down),
            same(22, tile(yd, xl, hi_a), right), same(23, tile(yd, xr, hi_b), left),
            same(24, tile(yu, xl, hi_a), right), same(25, tile(yu, xr, hi_b), left),
            same(26, tile(y, xl, hi_a), right), same(27, tile(y, xr, hi_b), left),
        ]

    def set_h():
        return [
            same(28, tile(yd, x2, lo_a), up), same(29, tile(yu, x2, lo_b), down),
            same(30, tile(y2, xl, hi_a), right), same(31, tile(y2, xr, hi_b), left),
        ]

    tiles = (
        (y, x),
        (y, xl), (y, xr), (yd, x), (yu, x), (yd, xl), (yd, xr), (yu, xl), (yu, xr),
        (y, x2), (y2, x), (yd, x2), (yu, x2), (y2, xl), (y2, xr),
        (y2, x2),
    )

    def owned_there(k, core_):
        y_, x_ = tiles[k]
        t = lax.rem(y_, 2) * 4 + x_
        owner = 2 * yh + core_
        lowest = jnp.where(owner == 0, 0, jnp.where(owner == 1, 1, jnp.where(owner == 2, 2, 5)))
        highest = jnp.where(owner == 0, 1, jnp.where(owner == 1, 4, jnp.where(owner == 2, 6, 7)))
        return (t >= lowest) & (t <= highest)

    def start_sibs(first, end):
        for k in range(first, end):
            pl.when(owned_there(k, 1 - core))(sib(k, tile(*tiles[k])).start)

    def arrived_sibs():
        for k in range(16):
            pl.when(owned_there(k, core))(sib(k, tile(*tiles[k])).wait_recv)

    def sent_sibs():
        for k in range(16):
            pl.when(owned_there(k, 1 - core))(sib(k, tile(*tiles[k])).wait_send)

    def start(copies):
        for c in copies:
            c.start()

    def arrived(copies):
        for c in copies:
            c.wait_recv()

    def gather_second():
        start(set_f())

    def gather_third():
        each(STEPS, lambda q: start(set_c(q)))
        start(set_d())

    def gather_fourth():
        arrived(set_b())

        @pl.when(section != last_section - 2)
        def _():
            arrived(set_f())
            each(STEPS, lambda q: start(set_e(q)))

        each(STEPS, lambda q: arrived(set_c(q)))
        arrived(set_d())
        start(set_g())
        start_sibs(1, 9)

    def gather_fifth():
        each(STEPS, lambda q: arrived(set_e(q)))
        arrived(set_g())
        start(set_h())
        start_sibs(9, 15)

    def gather_sixth():
        arrived(set_h())
        start_sibs(15, 16)

    turn(1)
    own_acts.wait()
    keep_own.start()

    @pl.when(section < last_section)
    def _():
        each(STEPS, lambda q: start(set_a(q)))
        start(set_b())
        start_sibs(0, 1)
        each(STEPS, lambda q: arrived(set_a(q)))
        start(set_f())

    @pl.when(section < last_section - 1)
    def _():
        gather_third()

    @pl.when(section == last_section - 2)
    def _():
        arrived(set_f())
        each(STEPS, lambda q: start(set_e(q)))

    @pl.when(is_first)
    def _():
        gather_fourth()
        gather_fifth()


    @pl.when(section < last_section)
    def _():
        turn(2)
        turn(3)

    own_gate.wait()
    gate_swaps[0].wait()

    @pl.when(is_last)
    def _():
        own_grad.wait()
        grad_swaps[0].wait()

    def rows_of(m):
        return pl.ds(pl.multiple_of(m * micro, micro), micro)

    def pre_swap(m):
        ref = pav.at[yh, :, rows_of(m), mine]
        return remote(ref, ref, pre_sem, (m,), sibling)

    def pre_across(m):
        ref = pav.at[yh, :, rows_of(m), mine]
        return remote(ref, ref, ag_sem, (m,), across)

    def send_a(m, k):
        return remote(part.at[m, k], got_a.at[m, k], a_sem, (m, k), (right, left)[k])

    def send_b(m, k):
        return remote(part.at[m, 2 + k], got_b.at[m, k], b_sem, (m, k), (right, left)[k])

    def send_same(m):
        return remote(part.at[m, 4 + yl], got_b.at[m, 2], b_sem, (m, 2), at(x + 1 - 2 * yl, y, section, core))

    def send_diagonal(m):
        return remote(part.at[m, 5 - yl], got_b.at[m, 3], b_sem, (m, 3), diagonal)

    def send_u(m, k):
        return remote((kept.at[m], part.at[m, 6])[k], got_u.at[m, k], u_sem, (m, k), (below_same, below_other)[k])

    def send_y(m):
        return remote(part.at[m, 6], got_y.at[m], y_sem, (m,), partner)

    def send_back(m, k):
        src = sums.at[(core, 1 - core)[k], rows_of(m), :]
        return remote(src, grads.at[rows_of(m), mine], back_sem, (m, k), (above_same, above_sibling)[k])

    def grad_own(m):
        return pltpu.make_async_copy(total.at[core, rows_of(m), :], grads.at[rows_of(m), mine], out_loc_sem.at[m])

    def grad_other(m):
        return remote(total.at[1 - core, rows_of(m), :], grads.at[rows_of(m), mine], out_sem, (m,), sibling)

    def product(m, k):
        pre = jnp.concatenate([pav[yh, 0, rows_of(m), :], pav[yh, 1, rows_of(m), :]], axis=0)
        value = jnp.dot(pre, wt[k], preferred_element_type=F32).astype(BF)
        part[m, 2 * k] = value[:, :half]
        part[m, 2 * k + 1] = value[:, half:]

    def forward_step(m):
        def merge(k):
            part[m, 4 + k] = (part[m, 4 + k].astype(F32) + got_a[m, k].astype(F32)).astype(BF)

        send_a(m, 0).wait_recv()
        send_a(m, 1).wait_recv()
        merge(1 - yl)
        send_diagonal(m).start()
        merge(yl)
        send_same(m).start()

    def partner_step(m):
        for k in range(2):
            send_b(m, k).wait_recv()
        part[m, 6] = (part[m, 6].astype(F32) + got_b[m, yl].astype(F32)).astype(BF)

        @pl.when(section > 0)
        def _():
            send_u(m, 1).start()

        @pl.when(is_first)
        def _():
            send_y(m).start()

    def reduce_step(m):
        send_same(m).wait_recv()
        send_diagonal(m).wait_recv()
        kept[m] = (
            (part[m, 7].astype(F32) + got_b[m, 1 - yl].astype(F32))
            + (got_b[m, 2].astype(F32) + got_b[m, 3].astype(F32))
        ).astype(BF)

        @pl.when(section > 0)
        def _():
            send_u(m, 0).start()

    def finish_step(m):
        send_y(m).wait_recv()
        value = (kept[m].astype(F32) + got_y[m].astype(F32)).astype(BF)
        total[0, rows_of(m), :] = value[:micro]
        total[1, rows_of(m), :] = value[micro:]
        grad_own(m).start()
        grad_other(m).start()

    def times_gate(m, upstream):
        pre = (upstream.astype(F32) * gv[:, rows_of(m), :].astype(F32)).astype(BF)
        pav[yh, :, rows_of(m), mine] = pre
        pre_swap(m).start()

    def take_step(m):
        @pl.when(is_last)
        def _():
            times_gate(m, ov[:, rows_of(m), :])

        @pl.when(section < last_section)
        def _():
            send_u(m, 0).wait_recv()
            send_u(m, 1).wait_recv()
            value = (got_u[m, 0].astype(F32) + got_u[m, 1].astype(F32)).astype(BF).reshape(2, micro, half)
            times_gate(m, value)
            sums[:, rows_of(m), :] = value

    def give_back(m):
        @pl.when(section < last_section)
        def _():
            for k in range(2):
                send_back(m, k).start()

    def step(m):
        take_step(m)
        pre_across(m).start()
        give_back(m)
        pre_swap(m).wait_recv()
        product(m, 0)
        send_a(m, 0).start()
        send_a(m, 1).start()


        @pl.when(m > 0)
        def _():
            product(m - 1, 2)
            forward_step(m - 1)


        @pl.when(m > 1)
        def _():
            reduce_step(m - 2)


        @pl.when(m > 0)
        def _():
            product(m - 1, 3)

        product(m, 1)
        send_b(m, 0).start()
        send_b(m, 1).start()


        @pl.when(m > 0)
        def _():
            partner_step(m - 1)


        @pl.when(m > 2)
        def _():
            pl.when(is_first)(lambda: finish_step(m - 3))

        pl.when(is_first & (m == 2))(gather_sixth)

        @pl.when(m == 0)
        def _():
            gate_swaps[1].wait()
            pl.when(is_last)(grad_swaps[1].wait)

        @pl.when(is_last & (m == 0))
        def _():
            turn(2)
            turn(3)


    fix_ref = pav.at[1 - yh, :, :, mine]
    fix = remote(fix_ref, fix_ref, fix_sem, (), sibling)

    def exchange_pre():
        each(STEPS, lambda m: pre_across(m).wait_recv())
        fix.start()
        fix.wait_recv()

    each(STEPS, step)
    product(STEPS - 1, 2)
    forward_step(STEPS - 1)
    reduce_step(STEPS - 2)
    product(STEPS - 1, 3)
    partner_step(STEPS - 1)

    @pl.when(is_first)
    def _():
        exchange_pre()
        arrived_sibs()

    reduce_step(STEPS - 1)

    @pl.when(is_last)
    def _():
        each(STEPS, lambda q: start(set_a(q)))
        start(set_b())
        start_sibs(0, 1)
        each(STEPS, lambda q: arrived(set_a(q)))
        start(set_f())
        gather_third()

    @pl.when(section == last_section - 1)
    def _():
        gather_third()

    @pl.when(section > 0)
    def _():
        gather_fourth()
        each(STEPS, lambda m: pre_across(m).wait_recv())
        fix.start()
        gather_fifth()
        gather_sixth()
        fix.wait_recv()
        arrived_sibs()

    @pl.when(is_first)
    def _():
        finish_step(STEPS - 3)
        finish_step(STEPS - 2)
        finish_step(STEPS - 1)

    def drain(m):
        pre_swap(m).wait_send()
        pre_across(m).wait_send()
        for k in range(2):
            send_a(m, k).wait_send()
        for k in range(2):
            send_b(m, k).wait_send()
        send_same(m).wait_send()
        send_diagonal(m).wait_send()
        for c in set_a(m) + set_c(m) + set_e(m):
            c.wait_send()

        @pl.when(section > 0)
        def _():
            for k in range(2):
                send_u(m, k).wait_send()
                send_back(m, k).wait_recv()

        @pl.when(section < last_section)
        def _():
            for k in range(2):
                send_back(m, k).wait_send()

        @pl.when(is_first)
        def _():
            send_y(m).wait_send()
            grad_own(m).wait()
            grad_other(m).wait()

    each(STEPS, drain)
    for c in set_b() + set_f() + set_d() + set_g() + set_h():
        c.wait_send()
    sent_sibs()
    fix.wait_send()
    keep_own.wait()


def run_window(weight, acts, gates, out_grad):
    tokens, width = acts.shape
    rows = weight.shape[0]
    half = width // 2
    dma = pltpu.SemaphoreType.DMA
    micro = 2 * tokens // STEPS
    hbm = pl.BlockSpec(memory_space=pl.ANY)
    return pl.pallas_call(
        window_kernel,
        out_shape=(
            pltpu.VMEM((tokens, width), BF),
            jax.ShapeDtypeStruct((2, 2, 4, 2, tokens, width), BF),
            pltpu.VMEM((2, 2, tokens, width), BF),
        ),
        in_specs=[hbm] * 4,
        out_specs=(pl.BlockSpec(memory_space=pltpu.VMEM), hbm, pl.BlockSpec(memory_space=pltpu.VMEM)),
        scratch_shapes=[
            pltpu.VMEM((tokens, width), BF),
            pltpu.VMEM((8, half, width), BF),
            pltpu.VMEM((4, width, width), BF),
            pltpu.VMEM((2, tokens, half), BF),
            pltpu.VMEM((2, tokens, half), BF),
            pltpu.VMEM((STEPS, 8, micro, half), BF),
            pltpu.VMEM((STEPS, 2, micro, half), BF),
            pltpu.VMEM((STEPS, 4, micro, half), BF),
            pltpu.VMEM((STEPS, 2, micro, half), BF),
            pltpu.VMEM((STEPS, micro, half), BF),
            pltpu.VMEM((STEPS, micro, half), BF),
            pltpu.VMEM((2, tokens, half), BF),
            pltpu.VMEM((2, tokens, half), BF),
            dma((8,)),
            dma((2, 2)),
            dma((2, 2)),
            dma((2, STEPS)),
            dma((2, STEPS, 2)),
            dma((2, STEPS, 4)),
            dma((2, STEPS, 2)),
            dma((2, STEPS)),
            dma((2, STEPS)),
            dma((2,)),
            dma((4,)),
            dma((STEPS,)),
            dma((2, STEPS)),
            dma((2, STEPS, 2)),
            dma((2, 3, STEPS, 4)),
            dma((2, 32)),
            dma((2, 16)),
        ],
        compiler_params=pltpu.CompilerParams(
            collective_id=0, has_side_effects=True, vmem_limit_bytes=60 * 2**20
        ),
        cost_estimate=pl.CostEstimate(
            flops=2 * tokens * width * rows,
            bytes_accessed=2 * rows * width,
            transcendentals=0,
        ),
        name="window",
    )(weight, acts, gates, out_grad)


def owned_kernel(owners, acts, pre, grads, owned, grads_out, held, stage, in_sem, out_sem, copy_sem):
    section, owner = lax.axis_index("section"), lax.axis_index("dp")
    tokens, width = pre.shape[2:]
    first = jnp.int32(0)
    for k in range(3):
        first = first + jnp.where(k < owner, owners[section, k], 0)
    count = owners[section, owner]
    blocks = held.shape[0]
    group = BLOCKS
    rows = group * OWN_BLK

    def load(b):
        block = jnp.clip(first + jnp.minimum(b, count - 1), 0, 63)
        lane = pl.ds(pl.multiple_of(lax.rem(block, 8) * OWN_BLK, OWN_BLK), OWN_BLK)
        src = acts.at[:, lax.div(block, 32), lax.rem(lax.div(block, 8), 4), :, :, lane]
        return pltpu.make_async_copy(src, held.at[b], in_sem.at[b])

    def out(i):
        part = pl.ds(pl.multiple_of(i * rows, rows), rows)
        return pltpu.make_async_copy(stage.at[part], owned.at[part], out_sem.at[i])

    def chunk(i):
        for k in range(group):
            load(group * i + k).wait()
        lhs = jnp.concatenate(
            [held[group * i + k].reshape(4 * tokens, OWN_BLK) for k in range(group)], axis=1
        )
        rhs = pre[...].reshape(4 * tokens, width)
        value = lax.dot_general(lhs, rhs, (((0,), (0,)), ((), ())), preferred_element_type=F32).astype(BF)
        for k in range(group):
            piece = value[k * OWN_BLK : (k + 1) * OWN_BLK]
            stage[pl.ds(pl.multiple_of(i * rows + k * OWN_BLK, OWN_BLK), OWN_BLK), :] = jnp.where(
                group * i + k < count, piece, jnp.zeros_like(piece)
            )
        out(i).start()

    each(blocks, lambda b: load(b).start())
    keep = pltpu.make_async_copy(grads, grads_out, copy_sem)
    keep.start()
    each(blocks // group, chunk)
    each(blocks // group, lambda i: out(i).wait())
    keep.wait()


def run_owned(owners, acts, pre, grads, cap):
    tokens, width = pre.shape[2:]
    hbm = pl.BlockSpec(memory_space=pl.ANY)
    blocks = cap // OWN_BLK
    return pl.pallas_call(
        owned_kernel,
        out_shape=(jax.ShapeDtypeStruct((cap, width), BF), jax.ShapeDtypeStruct(grads.shape, BF)),
        in_specs=[pl.BlockSpec(memory_space=pltpu.SMEM), hbm] + [pl.BlockSpec(memory_space=pltpu.VMEM)] * 2,
        out_specs=(hbm, hbm),
        scratch_shapes=[
            pltpu.VMEM((blocks, 2, 2, tokens, OWN_BLK), BF),
            pltpu.VMEM((cap, width), BF),
            pltpu.SemaphoreType.DMA((blocks,)),
            pltpu.SemaphoreType.DMA((blocks // BLOCKS,)),
            pltpu.SemaphoreType.DMA,
        ],
        compiler_params=pltpu.CompilerParams(vmem_limit_bytes=40 * 2**20),
        cost_estimate=pl.CostEstimate(
            flops=8 * cap * width * tokens, bytes_accessed=12 * cap * width, transcendentals=0
        ),
        name="owned",
    )(owners, acts, pre, grads)


def on_device(weights, acts, gates, out_grad, owner_rows):
    width = weights.shape[1]
    cap = 3 * width // (2 * lax.axis_size("dp"))
    tokens = acts.shape[1] * acts.shape[2]

    def flat(a):
        return a.reshape(tokens, a.shape[-1])

    grads, av, pav = run_window(weights[0], flat(acts[0]), flat(gates[0]), flat(out_grad))
    owned, grads = run_owned(owner_rows, av, pav, grads, cap)
    return owned[None, None], grads.reshape(acts.shape)


def solution(mesh):
    placed = (
        P("section", None, "tensor"),
        P("section", None, "dp", "tensor"),
        P("section", None, "dp", "tensor"),
        P(None, "dp", "tensor"),
        P(),
    )
    return jax.shard_map(
        on_device,
        mesh=mesh,
        in_specs=placed,
        out_specs=(P("section", "dp", None, "tensor"), P("section", None, "dp", "tensor")),
        check_vma=False,
    )
```

```python
import jax
import jax.numpy as jnp
from jax import lax
from jax.experimental import pallas as pl
from jax.experimental.pallas import tpu as pltpu
from jax.sharding import PartitionSpec as P

OWN_BLK = 128
BLOCKS = 4
STEPS = 8
MESH = pl.DeviceIdType.MESH
BF = jnp.bfloat16
F32 = jnp.float32


def remote(src, dst, sems, index, device):
    return pltpu.make_async_remote_copy(
        src_ref=src,
        dst_ref=dst,
        send_sem=sems.at[(0,) + index],
        recv_sem=sems.at[(1,) + index],
        device_id=device,
        device_id_type=MESH,
    )


def each(count, body):
    def wrapped(i, _):
        body(i)
        return 0

    lax.fori_loop(0, count, wrapped, 0)


def window_kernel(
    weight, acts, gates, out_grad,
    grads, av, pav,
    own, wv, wt, gv, ov, part, got_a, got_b, got_u, got_y, kept, total, sums,
    w_sem, gate_sem, og_sem, pre_sem, a_sem, b_sem, u_sem, y_sem, ag_sem, fix_sem, loc_sem,
    out_loc_sem, out_sem, back_sem, paced_sem, g_sem, sib_sem,
):
    section = lax.axis_index("section")
    tensor = lax.axis_index("tensor")
    dp = lax.axis_index("dp")
    last_section = lax.axis_size("section") - 1
    x, yl = lax.rem(tensor, 4), tensor // 4
    yh, core = dp // 2, lax.rem(dp, 2)
    y = yh * 2 + yl
    tokens, width = gates.shape
    micro = tokens // STEPS
    half = width // 2
    is_last = section == last_section
    is_first = section == 0

    def at(x_, y_, z_, core_):
        y_ = lax.rem(y_ + 4, 4)
        return (z_, lax.rem(y_, 2) * 4 + lax.rem(x_ + 4, 4), (y_ // 2) * 2 + core_)

    right, left = at(x + 1, y, section, core), at(x - 1, y, section, core)
    up, down = at(x, y + 1, section, core), at(x, y - 1, section, core)
    across = at(x, y + 2, section, core)
    sibling = at(x, y, section, 1 - core)
    other_y = yh * 2 + 1 - yl
    partner = at(x, other_y, section, core)
    diagonal = at(x - 1 + 2 * yl, other_y, section, core)
    below = lax.rem(section + last_section, last_section + 1)
    above = lax.rem(section + 1, last_section + 1)
    below_same, below_other = at(x, y, below, core), at(x, other_y, below, core)
    above_same, above_other = at(x, y, above, core), at(x, other_y, above, core)
    below_sibling, above_sibling = at(x, y, below, 1 - core), at(x, y, above, 1 - core)

    mine = pl.ds(pl.multiple_of(core * half, half), half)
    theirs = pl.ds(pl.multiple_of((1 - core) * half, half), half)

    own_gate = pltpu.make_async_copy(gates.at[:, mine], gv.at[core], loc_sem.at[0])
    own_gate.start()
    own_grad = pltpu.make_async_copy(out_grad.at[:, mine], ov.at[core], loc_sem.at[2])
    pl.when(is_last)(own_grad.start)

    places = (
        (2, 0), (2, 1), (1, 1), (3, 0), (1, 0), (3, 1), (0, 1 - yl), (0, yl),
    )
    loads = []
    for k, (dx, l) in enumerate(places):
        start = (l * 4 + lax.rem(x + dx, 4)) * 1024 + core * half
        load = pltpu.make_async_copy(
            weight.at[pl.ds(pl.multiple_of(start, half), half), :], wv.at[k], w_sem.at[k]
        )
        load.start()
        loads.append(load)
    own_acts = pltpu.make_async_copy(acts, own, loc_sem.at[1])
    keep_own = pltpu.make_async_copy(own, av.at[yh, yl, x, core], loc_sem.at[3])
    own_acts.start()

    barrier = pltpu.get_barrier_semaphore()
    neighbours = (
        right, left, up, down, across, diagonal, sibling, below_same, below_other, below_sibling,
        above_same, above_other, above_sibling,
    )
    for device in neighbours:
        pl.semaphore_signal(barrier, inc=1, device_id=device, device_id_type=MESH)

    def turn(k):
        for j in range(2):
            loads[2 * k + j].wait()
            wt[k, :, j * half : (j + 1) * half] = wv[2 * k + j].T

    turn(0)
    pl.semaphore_wait(barrier, len(neighbours))

    first_rows, later_rows = pl.ds(0, micro), pl.ds(micro, tokens - micro)

    def swap(src, dst, sems, k, rows):
        return remote(src.at[rows, theirs], dst.at[core, rows], sems, (k,), sibling)

    gate_swaps = [swap(gates, gv, gate_sem, k, rows) for k, rows in enumerate((first_rows, later_rows))]
    grad_swaps = [swap(out_grad, ov, og_sem, k, rows) for k, rows in enumerate((first_rows, later_rows))]
    gate_swaps[0].start()
    pl.when(is_last)(grad_swaps[0].start)
    gate_swaps[1].start()
    pl.when(is_last)(grad_swaps[1].start)

    tok = tokens // 2
    lo, hi = pl.ds(0, tok), pl.ds(tok, tok)
    lo_a, lo_b = pl.ds(0, tok // 2), pl.ds(tok // 2, tok // 2)
    hi_a, hi_b = pl.ds(tok, tok // 2), pl.ds(tok + tok // 2, tok // 2)
    xr, xl, x2 = lax.rem(x + 1, 4), lax.rem(x + 3, 4), lax.rem(x + 2, 4)
    yu, yd, y2 = lax.rem(y + 1, 4), lax.rem(y + 3, 4), lax.rem(y + 2, 4)
    piece = tok // STEPS

    def tile(y_, x_, rows=None):
        ref = av.at[y_ // 2, lax.rem(y_, 2), x_, core]
        return ref if rows is None else ref.at[rows]

    def same(k, ref, device):
        return remote(ref, ref, g_sem, (k,), device)

    def sib(k, ref):
        return remote(own if k == 0 else ref, ref, sib_sem, (k,), sibling)

    def paced(which, q, y_lo, x_lo, y_hi, x_hi, to_lo, to_hi):
        rows_lo = pl.ds(pl.multiple_of(q * piece, piece), piece)
        rows_hi = pl.ds(pl.multiple_of(tok + q * piece, piece), piece)
        ref_lo, ref_hi = tile(y_lo, x_lo, rows_lo), tile(y_hi, x_hi, rows_hi)
        src_lo, src_hi = (own.at[rows_lo], own.at[rows_hi]) if which == 0 else (ref_lo, ref_hi)
        return [
            remote(src, ref, paced_sem, (which, q, k), device)
            for k, (src, ref, device) in enumerate(
                [
                    (src_lo, ref_lo, to_lo[0]), (src_lo, ref_lo, to_lo[1]),
                    (src_hi, ref_hi, to_hi[0]), (src_hi, ref_hi, to_hi[1]),
                ]
            )
        ]

    def set_a(q):
        return paced(0, q, y, x, y, x, (right, left), (up, down))

    def set_c(q):
        return paced(1, q, y, xl, yd, x, (up, down), (right, left))

    def set_b():
        return [
            remote(own.at[rows], tile(y, x, rows), g_sem, (k,), device)
            for k, (rows, device) in enumerate([(lo, up), (lo, down), (hi, right), (hi, left)])
        ]

    def set_f():
        return [
            same(4, tile(y, xl, lo_a), right), same(5, tile(y, xr, lo_b), left),
            same(6, tile(yd, x, hi_a), up), same(7, tile(yu, x, hi_b), down),
        ]

    def set_d():
        right_lo, up_hi = tile(y, xr, lo), tile(yu, x, hi)
        return [same(8, right_lo, up), same(9, right_lo, down), same(10, up_hi, right), same(11, up_hi, left)]

    def set_e(q):
        return paced(2, q, y, x2, y2, x, (up, down), (right, left))

    def set_g():
        return [
            same(16, tile(yd, xl, lo_a), up), same(17, tile(yu, xl, lo_b), down),
            same(18, tile(yd, xr, lo_a), up), same(19, tile(yu, xr, lo_b), down),
            same(20, tile(yd, x, lo_a), up), same(21, tile(yu, x, lo_b), down),
            same(22, tile(yd, xl, hi_a), right), same(23, tile(yd, xr, hi_b), left),
            same(24, tile(yu, xl, hi_a), right), same(25, tile(yu, xr, hi_b), left),
            same(26, tile(y, xl, hi_a), right), same(27, tile(y, xr, hi_b), left),
        ]

    def set_h():
        return [
            same(28, tile(yd, x2, lo_a), up), same(29, tile(yu, x2, lo_b), down),
            same(30, tile(y2, xl, hi_a), right), same(31, tile(y2, xr, hi_b), left),
        ]

    tiles = (
        (y, x),
        (y, xl), (y, xr), (yd, x), (yu, x), (yd, xl), (yd, xr), (yu, xl), (yu, xr),
        (y, x2), (y2, x), (yd, x2), (yu, x2), (y2, xl), (y2, xr),
        (y2, x2),
    )

    def owned_there(k, core_):
        y_, x_ = tiles[k]
        t = lax.rem(y_, 2) * 4 + x_
        owner = 2 * yh + core_
        lowest = jnp.where(owner == 0, 0, jnp.where(owner == 1, 1, jnp.where(owner == 2, 2, 5)))
        highest = jnp.where(owner == 0, 1, jnp.where(owner == 1, 4, jnp.where(owner == 2, 6, 7)))
        return (t >= lowest) & (t <= highest)

    def start_sibs(first, end):
        for k in range(first, end):
            pl.when(owned_there(k, 1 - core))(sib(k, tile(*tiles[k])).start)

    def arrived_sibs():
        for k in range(16):
            pl.when(owned_there(k, core))(sib(k, tile(*tiles[k])).wait_recv)

    def sent_sibs():
        for k in range(16):
            pl.when(owned_there(k, 1 - core))(sib(k, tile(*tiles[k])).wait_send)

    def start(copies):
        for c in copies:
            c.start()

    def arrived(copies):
        for c in copies:
            c.wait_recv()

    def gather_second():
        start(set_f())

    def gather_third():
        each(STEPS, lambda q: start(set_c(q)))
        start(set_d())

    def gather_fourth():
        arrived(set_b())

        @pl.when(section != last_section - 2)
        def _():
            arrived(set_f())
            each(STEPS, lambda q: start(set_e(q)))

        each(STEPS, lambda q: arrived(set_c(q)))
        arrived(set_d())
        start(set_g())
        start_sibs(1, 9)

    def gather_fifth():
        each(STEPS, lambda q: arrived(set_e(q)))
        arrived(set_g())
        start(set_h())
        start_sibs(9, 15)

    def gather_sixth():
        arrived(set_h())
        start_sibs(15, 16)

    turn(1)
    own_acts.wait()
    keep_own.start()

    @pl.when(section < last_section)
    def _():
        each(STEPS, lambda q: start(set_a(q)))
        start(set_b())
        start_sibs(0, 1)
        each(STEPS, lambda q: arrived(set_a(q)))
        start(set_f())

    @pl.when(section < last_section - 1)
    def _():
        gather_third()

    @pl.when(section == last_section - 2)
    def _():
        arrived(set_f())
        each(STEPS, lambda q: start(set_e(q)))

    @pl.when(is_first)
    def _():
        gather_fourth()
        gather_fifth()


    @pl.when(section < last_section)
    def _():
        turn(2)
        turn(3)

    own_gate.wait()
    gate_swaps[0].wait()

    @pl.when(is_last)
    def _():
        own_grad.wait()
        grad_swaps[0].wait()

    def rows_of(m):
        return pl.ds(pl.multiple_of(m * micro, micro), micro)

    def pre_swap(m):
        ref = pav.at[yh, :, rows_of(m), mine]
        return remote(ref, ref, pre_sem, (m,), sibling)

    def pre_across(m):
        ref = pav.at[yh, :, rows_of(m), mine]
        return remote(ref, ref, ag_sem, (m,), across)

    def send_a(m, k):
        return remote(part.at[m, k], got_a.at[m, k], a_sem, (m, k), (right, left)[k])

    def send_b(m, k):
        return remote(part.at[m, 2 + k], got_b.at[m, k], b_sem, (m, k), (right, left)[k])

    def send_same(m):
        return remote(part.at[m, 4 + yl], got_b.at[m, 2], b_sem, (m, 2), at(x + 1 - 2 * yl, y, section, core))

    def send_diagonal(m):
        return remote(part.at[m, 5 - yl], got_b.at[m, 3], b_sem, (m, 3), diagonal)

    def send_u(m, k):
        return remote((kept.at[m], part.at[m, 6])[k], got_u.at[m, k], u_sem, (m, k), (below_same, below_other)[k])

    def send_y(m):
        return remote(part.at[m, 6], got_y.at[m], y_sem, (m,), partner)

    def send_back(m, k):
        src = sums.at[(core, 1 - core)[k], rows_of(m), :]
        return remote(src, grads.at[rows_of(m), mine], back_sem, (m, k), (above_same, above_sibling)[k])

    def grad_own(m):
        return pltpu.make_async_copy(total.at[core, rows_of(m), :], grads.at[rows_of(m), mine], out_loc_sem.at[m])

    def grad_other(m):
        return remote(total.at[1 - core, rows_of(m), :], grads.at[rows_of(m), mine], out_sem, (m,), sibling)

    def product(m, k):
        pre = jnp.concatenate([pav[yh, 0, rows_of(m), :], pav[yh, 1, rows_of(m), :]], axis=0)
        value = jnp.dot(pre, wt[k], preferred_element_type=F32).astype(BF)
        part[m, 2 * k] = value[:, :half]
        part[m, 2 * k + 1] = value[:, half:]

    def forward_step(m):
        def merge(k):
            part[m, 4 + k] = (part[m, 4 + k].astype(F32) + got_a[m, k].astype(F32)).astype(BF)

        send_a(m, 0).wait_recv()
        send_a(m, 1).wait_recv()
        merge(1 - yl)
        send_diagonal(m).start()
        merge(yl)
        send_same(m).start()

    def partner_step(m):
        for k in range(2):
            send_b(m, k).wait_recv()
        part[m, 6] = (part[m, 6].astype(F32) + got_b[m, yl].astype(F32)).astype(BF)

        @pl.when(section > 0)
        def _():
            send_u(m, 1).start()

        @pl.when(is_first)
        def _():
            send_y(m).start()

    def reduce_step(m):
        send_same(m).wait_recv()
        send_diagonal(m).wait_recv()
        kept[m] = (
            (part[m, 7].astype(F32) + got_b[m, 1 - yl].astype(F32))
            + (got_b[m, 2].astype(F32) + got_b[m, 3].astype(F32))
        ).astype(BF)

        @pl.when(section > 0)
        def _():
            send_u(m, 0).start()

    def finish_step(m):
        send_y(m).wait_recv()
        value = (kept[m].astype(F32) + got_y[m].astype(F32)).astype(BF)
        total[0, rows_of(m), :] = value[:micro]
        total[1, rows_of(m), :] = value[micro:]
        grad_own(m).start()
        grad_other(m).start()

    def times_gate(m, upstream):
        pre = (upstream.astype(F32) * gv[:, rows_of(m), :].astype(F32)).astype(BF)
        pav[yh, :, rows_of(m), mine] = pre
        pre_swap(m).start()

    def take_step(m):
        @pl.when(is_last)
        def _():
            times_gate(m, ov[:, rows_of(m), :])

        @pl.when(section < last_section)
        def _():
            send_u(m, 0).wait_recv()
            send_u(m, 1).wait_recv()
            value = (got_u[m, 0].astype(F32) + got_u[m, 1].astype(F32)).astype(BF).reshape(2, micro, half)
            times_gate(m, value)
            sums[:, rows_of(m), :] = value

    def give_back(m):
        @pl.when(section < last_section)
        def _():
            for k in range(2):
                send_back(m, k).start()

    def step(m):
        take_step(m)
        pre_across(m).start()
        give_back(m)
        pre_swap(m).wait_recv()
        product(m, 0)
        send_a(m, 0).start()
        send_a(m, 1).start()

        @pl.when(m > 0)
        def _():
            product(m - 1, 2)
            forward_step(m - 1)
            product(m - 1, 3)


        @pl.when(m > 1)
        def _():
            reduce_step(m - 2)

        product(m, 1)
        send_b(m, 0).start()
        send_b(m, 1).start()

        @pl.when(m > 0)
        def _():
            partner_step(m - 1)


        @pl.when(m > 2)
        def _():
            pl.when(is_first)(lambda: finish_step(m - 3))

        pl.when(is_first & (m == 2))(gather_sixth)

        @pl.when(m == 0)
        def _():
            gate_swaps[1].wait()
            pl.when(is_last)(grad_swaps[1].wait)

        @pl.when(is_last & (m == 0))
        def _():
            turn(2)
            turn(3)


    fix_ref = pav.at[1 - yh, :, :, mine]
    fix = remote(fix_ref, fix_ref, fix_sem, (), sibling)

    def exchange_pre():
        each(STEPS, lambda m: pre_across(m).wait_recv())
        fix.start()

    def drain_step(m):
        pre_swap(m).wait_send()
        pre_across(m).wait_send()
        for k in range(2):
            send_a(m, k).wait_send()
            send_b(m, k).wait_send()
        send_same(m).wait_send()
        send_diagonal(m).wait_send()

        @pl.when(section > 0)
        def _():
            for k in range(2):
                send_u(m, k).wait_send()
                send_back(m, k).wait_recv()

        @pl.when(section < last_section)
        def _():
            for k in range(2):
                send_back(m, k).wait_send()

        @pl.when(is_first)
        def _():
            send_y(m).wait_send()
            grad_own(m).wait()
            grad_other(m).wait()

    def drain_gather():
        def paced_out(q):
            for c in set_a(q) + set_c(q) + set_e(q):
                c.wait_send()

        each(STEPS, paced_out)
        for c in set_b() + set_f() + set_d() + set_g():
            c.wait_send()
        keep_own.wait()

    def drain_last():
        for c in set_h():
            c.wait_send()
        sent_sibs()

    each(STEPS, step)
    product(STEPS - 1, 2)
    forward_step(STEPS - 1)
    product(STEPS - 1, 3)
    reduce_step(STEPS - 2)
    partner_step(STEPS - 1)

    @pl.when(is_first)
    def _():
        exchange_pre()
        finish_step(STEPS - 3)
        finish_step(STEPS - 2)
        arrived_sibs()
        drain_gather()
        drain_last()
        each(STEPS - 1, drain_step)

    reduce_step(STEPS - 1)

    @pl.when(is_first)
    def _():
        finish_step(STEPS - 1)

    @pl.when(is_last)
    def _():
        each(STEPS, lambda q: start(set_a(q)))
        start(set_b())
        start_sibs(0, 1)
        each(STEPS, lambda q: arrived(set_a(q)))
        start(set_f())
        gather_third()

    @pl.when(section == last_section - 1)
    def _():
        gather_third()

    @pl.when(section > 0)
    def _():
        gather_fourth()
        exchange_pre()
        each(STEPS - 1, drain_step)
        gather_fifth()
        drain_gather()
        gather_sixth()
        arrived_sibs()
        drain_last()

    fix.wait()
    drain_step(STEPS - 1)


def run_window(weight, acts, gates, out_grad):
    tokens, width = acts.shape
    rows = weight.shape[0]
    half = width // 2
    dma = pltpu.SemaphoreType.DMA
    micro = 2 * tokens // STEPS
    hbm = pl.BlockSpec(memory_space=pl.ANY)
    return pl.pallas_call(
        window_kernel,
        out_shape=(
            pltpu.VMEM((tokens, width), BF),
            jax.ShapeDtypeStruct((2, 2, 4, 2, tokens, width), BF),
            pltpu.VMEM((2, 2, tokens, width), BF),
        ),
        in_specs=[hbm] * 4,
        out_specs=(pl.BlockSpec(memory_space=pltpu.VMEM), hbm, pl.BlockSpec(memory_space=pltpu.VMEM)),
        scratch_shapes=[
            pltpu.VMEM((tokens, width), BF),
            pltpu.VMEM((8, half, width), BF),
            pltpu.VMEM((4, width, width), BF),
            pltpu.VMEM((2, tokens, half), BF),
            pltpu.VMEM((2, tokens, half), BF),
            pltpu.VMEM((STEPS, 8, micro, half), BF),
            pltpu.VMEM((STEPS, 2, micro, half), BF),
            pltpu.VMEM((STEPS, 4, micro, half), BF),
            pltpu.VMEM((STEPS, 2, micro, half), BF),
            pltpu.VMEM((STEPS, micro, half), BF),
            pltpu.VMEM((STEPS, micro, half), BF),
            pltpu.VMEM((2, tokens, half), BF),
            pltpu.VMEM((2, tokens, half), BF),
            dma((8,)),
            dma((2, 2)),
            dma((2, 2)),
            dma((2, STEPS)),
            dma((2, STEPS, 2)),
            dma((2, STEPS, 4)),
            dma((2, STEPS, 2)),
            dma((2, STEPS)),
            dma((2, STEPS)),
            dma((2,)),
            dma((4,)),
            dma((STEPS,)),
            dma((2, STEPS)),
            dma((2, STEPS, 2)),
            dma((2, 3, STEPS, 4)),
            dma((2, 32)),
            dma((2, 16)),
        ],
        compiler_params=pltpu.CompilerParams(
            collective_id=0, has_side_effects=True, vmem_limit_bytes=60 * 2**20
        ),
        cost_estimate=pl.CostEstimate(
            flops=2 * tokens * width * rows,
            bytes_accessed=2 * rows * width,
            transcendentals=0,
        ),
        name="window",
    )(weight, acts, gates, out_grad)


def owned_kernel(owners, acts, pre, grads, owned, grads_out, held, stage, in_sem, out_sem, copy_sem):
    section, owner = lax.axis_index("section"), lax.axis_index("dp")
    tokens, width = pre.shape[2:]
    first = jnp.int32(0)
    for k in range(3):
        first = first + jnp.where(k < owner, owners[section, k], 0)
    count = owners[section, owner]
    blocks = held.shape[0]
    group = BLOCKS
    rows = group * OWN_BLK

    def load(b):
        block = jnp.clip(first + jnp.minimum(b, count - 1), 0, 63)
        lane = pl.ds(pl.multiple_of(lax.rem(block, 8) * OWN_BLK, OWN_BLK), OWN_BLK)
        src = acts.at[:, lax.div(block, 32), lax.rem(lax.div(block, 8), 4), :, :, lane]
        return pltpu.make_async_copy(src, held.at[b], in_sem.at[b])

    def out(i):
        part = pl.ds(pl.multiple_of(i * rows, rows), rows)
        return pltpu.make_async_copy(stage.at[part], owned.at[part], out_sem.at[i])

    def chunk(i):
        for k in range(group):
            load(group * i + k).wait()
        lhs = jnp.concatenate(
            [held[group * i + k].reshape(4 * tokens, OWN_BLK) for k in range(group)], axis=1
        )
        rhs = pre[...].reshape(4 * tokens, width)
        value = lax.dot_general(lhs, rhs, (((0,), (0,)), ((), ())), preferred_element_type=F32).astype(BF)
        for k in range(group):
            piece = value[k * OWN_BLK : (k + 1) * OWN_BLK]
            stage[pl.ds(pl.multiple_of(i * rows + k * OWN_BLK, OWN_BLK), OWN_BLK), :] = jnp.where(
                group * i + k < count, piece, jnp.zeros_like(piece)
            )
        out(i).start()

    each(blocks, lambda b: load(b).start())
    keep = pltpu.make_async_copy(grads, grads_out, copy_sem)
    keep.start()
    each(blocks // group, chunk)
    each(blocks // group, lambda i: out(i).wait())
    keep.wait()


def run_owned(owners, acts, pre, grads, cap):
    tokens, width = pre.shape[2:]
    hbm = pl.BlockSpec(memory_space=pl.ANY)
    blocks = cap // OWN_BLK
    return pl.pallas_call(
        owned_kernel,
        out_shape=(jax.ShapeDtypeStruct((cap, width), BF), jax.ShapeDtypeStruct(grads.shape, BF)),
        in_specs=[pl.BlockSpec(memory_space=pltpu.SMEM), hbm] + [pl.BlockSpec(memory_space=pltpu.VMEM)] * 2,
        out_specs=(hbm, hbm),
        scratch_shapes=[
            pltpu.VMEM((blocks, 2, 2, tokens, OWN_BLK), BF),
            pltpu.VMEM((cap, width), BF),
            pltpu.SemaphoreType.DMA((blocks,)),
            pltpu.SemaphoreType.DMA((blocks // BLOCKS,)),
            pltpu.SemaphoreType.DMA,
        ],
        compiler_params=pltpu.CompilerParams(vmem_limit_bytes=40 * 2**20),
        cost_estimate=pl.CostEstimate(
            flops=8 * cap * width * tokens, bytes_accessed=12 * cap * width, transcendentals=0
        ),
        name="owned",
    )(owners, acts, pre, grads)


def on_device(weights, acts, gates, out_grad, owner_rows):
    width = weights.shape[1]
    cap = 3 * width // (2 * lax.axis_size("dp"))
    tokens = acts.shape[1] * acts.shape[2]

    def flat(a):
        return a.reshape(tokens, a.shape[-1])

    grads, av, pav = run_window(weights[0], flat(acts[0]), flat(gates[0]), flat(out_grad))
    owned, grads = run_owned(owner_rows, av, pav, grads, cap)
    return owned[None, None], grads.reshape(acts.shape)


def solution(mesh):
    placed = (
        P("section", None, "tensor"),
        P("section", None, "dp", "tensor"),
        P("section", None, "dp", "tensor"),
        P(None, "dp", "tensor"),
        P(),
    )
    return jax.shard_map(
        on_device,
        mesh=mesh,
        in_specs=placed,
        out_specs=(P("section", "dp", None, "tensor"), P("section", None, "dp", "tensor")),
        check_vma=False,
    )
```
